256 devices in a mesh: scen: 32 (over y, x, core), col: 8 (over z).
Axes of the slice: x: 4, y: 4, z: 8, core: 2. Of those that a mesh axis runs over, the one named last changes fastest.
Arguments:
- inverses: float32 [32, 1024, 1024], P('scen'), as said below
- coupling: float32 [32, 1024, 8192], P('scen', None, 'col'), may hold values from -0.1875 to 0.1875
- tile_mask: int32 [32, 8], P('scen'), may hold values 0 or 1
- hess_diag: float32 [512], replicated, may hold values from 1 to 16
Outputs:
- factor: float32 [8192, 512], P(('col', 'scen'))
The draws below stay inside these ranges and needn't reach their ends.
Inputs may be any that keep to these rules, and one draw needn't show every extreme that they name: `inverses`: each scenario's matrix is symmetric and positive definite.
All inputs are finite; a program needn't handle non-finite values. No bound on the sum of `tile_mask` on one device may be relied on, other than what follows from the above.
Results may differ from the reference program's by a relative error of at most 0.0001.
Values sent between devices are 32-bit elements; how exact they have to be, the bound alone decides.
A program may use at most 64 MiB of HBM per device.

```python
import math
import jax
import jax.numpy as jnp
from jax import lax

NS = 1024
TILE = 128
PW = 256
NT = 8
NF = 8192
SCEN = 32


def draw_inverses(key, part):
    first = jax.random.fold_in(key, 11)
    second = jax.random.fold_in(key, 12)
    diagonal = jax.random.uniform(first, (SCEN, NS), jnp.float32, 1.0, 2.0)
    noise = jax.random.normal(second, (SCEN, NS, NS), jnp.float32)
    noise = noise * (0.3 / NS ** 0.5)
    sym = (noise + jnp.swapaxes(noise, 1, 2)) * 0.5 ** 0.5
    eye = jnp.eye(NS, dtype=jnp.float32)
    return sym + diagonal[:, :, None] * eye[None, :, :]


def set_ends(entries, rng, smallest, largest):
    extent = entries.shape
    index_at = [jax.random.randint(jax.random.fold_in(rng, axis), (), 0, extent[axis]) for axis in range(len(extent))]
    entries = entries.at[tuple(index_at)].set(smallest)
    longest = extent.index(max(extent))
    index_at[longest] = (index_at[longest] + 1) % extent[longest]
    return entries.at[tuple(index_at)].set(largest)


def block_scale(rng, shape, pieces, least, largest):
    loudness = 1.0
    for axis_at, parts in pieces:
        steps = jax.random.uniform(jax.random.fold_in(jax.random.fold_in(rng, 6), axis_at), (parts,), jnp.float32, least / len(pieces), largest / len(pieces))
        loudness = loudness * jnp.repeat(jnp.exp(steps), shape[axis_at] // parts).reshape((-1,) + (1,) * (len(shape) - 1 - axis_at))
    return loudness


def bell_draw(stream_key, extent, deviation, limit, pieces=(), kind=jnp.bfloat16):
    drawn = deviation * jax.random.normal(stream_key, extent, jnp.float32)
    if pieces:
        drawn = drawn * block_scale(stream_key, extent, pieces, -0.22, 0.18)
    return jnp.clip(drawn, -limit, limit).astype(kind)


def setup_inputs(seed: int = 0) -> dict:
    seeds = jax.random.split(jax.random.key(seed), 5)
    inverses = draw_inverses(jax.random.fold_in(seeds[4], 71), 0)
    coupling = bell_draw(seeds[1], (SCEN, NS, NF), NS ** -0.5, 0.1875, ((0, 32), (2, 8)), jnp.float32)
    tile_mask = set_ends((jax.random.randint(seeds[2], (SCEN, NT), 0, 4) < 3).astype(jnp.int32), jax.random.fold_in(seeds[2], 1), 0, 1)
    hess_diag = jnp.clip(jnp.exp(jax.random.uniform(seeds[3], (2 * PW,), jnp.float32, math.log(1.0), math.log(16.0))), 1.0, 16.0)
    return dict(inverses=inverses, coupling=coupling, tile_mask=tile_mask, hess_diag=hess_diag)


def reference(inverses, coupling, tile_mask, hess_diag):
    width = 2 * PW
    highest = lax.Precision.HIGHEST

    def add_one(total, item):
        inverse, block, keep = item
        row_keep = jnp.repeat(keep.astype(jnp.float32), TILE)
        masked = block * row_keep[:, None]
        product = jnp.dot(inverse.astype(jnp.float32), masked[:, :width].astype(jnp.float32), precision=highest, preferred_element_type=jnp.float32)
        contrib = lax.dot_general(masked.astype(jnp.float32), product.astype(jnp.float32), (((0,), (0,)), ((), ())), precision=highest, preferred_element_type=jnp.float32)
        return (total + contrib, None)
    schur, _ = lax.scan(add_one, jnp.zeros((NF, width), jnp.float32), (inverses, coupling, tile_mask))
    diag_index = jnp.arange(width)
    schur = schur.at[diag_index, diag_index].add(hess_diag)
    row_index = jnp.arange(NF)[:, None]
    chol1 = jnp.linalg.cholesky(schur[:PW, :PW])
    inv1 = jax.scipy.linalg.solve_triangular(chol1, jnp.eye(PW, dtype=jnp.float32), lower=True)
    lcol1 = jnp.dot(schur[:, :PW].astype(jnp.float32), inv1.T.astype(jnp.float32), precision=highest, preferred_element_type=jnp.float32)
    padded1 = jnp.concatenate([chol1, jnp.zeros((NF - PW, PW), jnp.float32)], axis=0)
    lcol1 = jnp.where(row_index < PW, padded1, lcol1)
    lower_b = lcol1[PW:width]
    update = schur[PW:width, PW:] - jnp.dot(lower_b.astype(jnp.float32), lower_b.T.astype(jnp.float32), precision=highest, preferred_element_type=jnp.float32)
    chol2 = jnp.linalg.cholesky(update)
    inv2 = jax.scipy.linalg.solve_triangular(chol2, jnp.eye(PW, dtype=jnp.float32), lower=True)
    rest = schur[:, PW:] - jnp.dot(lcol1.astype(jnp.float32), lower_b.T.astype(jnp.float32), precision=highest, preferred_element_type=jnp.float32)
    lcol2 = jnp.dot(rest.astype(jnp.float32), inv2.T.astype(jnp.float32), precision=highest, preferred_element_type=jnp.float32)
    padded2 = jnp.concatenate([jnp.zeros((PW, PW), jnp.float32), chol2, jnp.zeros((NF - width, PW), jnp.float32)], axis=0)
    lcol2 = jnp.where(row_index < width, padded2, lcol2)
    return jnp.concatenate([lcol1, lcol2], axis=1)
```

```python
import functools

import jax
import jax.numpy as jnp
from jax import lax
from jax.experimental import pallas as pl
from jax.experimental.pallas import tpu as pltpu
from jax.sharding import PartitionSpec as P


def filled_up(lines, size):
    spare = -lines.shape[0] % size
    if not spare:
        return lines
    return jnp.concatenate([lines, jnp.zeros((spare, *lines.shape[1:]), lines.dtype)])


def spread(x, axis, root):
    lines = jnp.where(lax.axis_index(axis) == root, x, jnp.zeros_like(x)).reshape(
        -1, *x.shape[1:][-1:]
    )
    padded = filled_up(lines, lax.axis_size(axis))
    own = lax.psum_scatter(padded, axis, scatter_dimension=0, tiled=True)
    return lax.all_gather(own, axis, axis=0, tiled=True)[: len(lines)].reshape(x.shape)


def in_blocks(x, dim, size):
    lengths = x.shape
    blocks = x.reshape(*lengths[:dim], size, lengths[dim] // size, *lengths[dim + 1 :])
    return jnp.moveaxis(blocks, dim, 0)


def sum_at_owner(x, axis, dim):
    size = lax.axis_size(axis)
    blocks = lax.all_to_all(in_blocks(x, dim, size), axis, 0, 0, tiled=True)
    return jnp.sum(blocks, axis=0)


def sent_to_all(x, axis):
    size = lax.axis_size(axis)
    return lax.all_to_all(jnp.broadcast_to(x[None], (size, *x.shape)), axis, 0, 0, tiled=True)


def in_order(blocks, dim):
    lengths = list(blocks.shape[1:])
    lengths[dim] *= blocks.shape[0]
    return jnp.moveaxis(blocks, 0, dim).reshape(lengths)


def collect(x, axis, dim):
    blocks = sent_to_all(x, axis)
    return in_order(blocks, dim)


def from_root(x, axis, root):
    return lax.dynamic_index_in_dim(lax.all_gather(x, axis), root, 0, keepdims=False)


def outer_rows(left, piece):
    return lax.dot_general(
        left,
        piece,
        (((0,), (0,)), ((), ())),
        precision=lax.Precision.HIGHEST,
        preferred_element_type=jnp.float32,
    )


def matmul(left, right):
    return jnp.dot(left, right, precision=lax.Precision.HIGHEST, preferred_element_type=jnp.float32)


def direct_body(inverses, coupling, tile_mask, hess_diag):
    inverse = inverses[0]
    local = coupling[0]
    width = hess_diag.shape[0]
    half = width // 2
    scen_size = lax.axis_size("scen")
    rows = local.shape[1] // scen_size
    row_keep = jnp.repeat(tile_mask[0].astype(jnp.float32), local.shape[0] // tile_mask.shape[1])
    panel = spread(local[:, :width], "col", 0)
    panel = panel * row_keep[:, None]
    product = matmul(inverse, panel) * row_keep[:, None]
    block = local
    summed = sum_at_owner(outer_rows(block, product), "scen", 0)
    first = lax.axis_index("col") * local.shape[1] + lax.axis_index("scen") * rows
    global_rows = first + jnp.arange(rows, dtype=jnp.int32)
    columns = jnp.arange(width, dtype=jnp.int32)
    schur = summed + jnp.where(columns[None, :] == global_rows[:, None], hess_diag[None, :], 0.0)

    def fetch(stacked, low):
        whole = collect(stacked, "scen", 1)
        block = whole[:, low : low + half]
        return from_root(block, "col", 0)

    identity = jnp.eye(half, dtype=jnp.float32)
    block_one = fetch(schur[None, :, :half], 0)[0]
    chol1 = jnp.linalg.cholesky(block_one)
    inv1 = jax.scipy.linalg.solve_triangular(chol1, identity, lower=True)
    lcol1 = matmul(schur[:, :half], inv1.T)
    own_one = lax.dynamic_slice_in_dim(chol1, jnp.clip(first, 0, half - rows), rows, 0)
    lcol1 = jnp.where(first < half, own_one, lcol1)
    paired = fetch(jnp.stack([schur[:, half:], lcol1]), half)
    lower_b = paired[1]
    update = paired[0] - matmul(lower_b, lower_b.T)
    chol2 = jnp.linalg.cholesky(update)
    inv2 = jax.scipy.linalg.solve_triangular(chol2, identity, lower=True)
    remain = schur[:, half:] - matmul(lcol1, lower_b.T)
    lcol2 = matmul(remain, inv2.T)
    own_two = lax.dynamic_slice_in_dim(chol2, jnp.clip(first - half, 0, half - rows), rows, 0)
    lcol2 = jnp.where(first < width, own_two, lcol2)
    lcol2 = jnp.where(first < half, jnp.zeros_like(lcol2), lcol2)
    return jnp.concatenate([lcol1, lcol2], axis=1)


F32 = jnp.float32
BF16 = jnp.bfloat16
STEPS = 3
SETTLED = 1.6e-5


def split(x):
    high = x.astype(BF16)
    return high, (x - high.astype(F32)).astype(BF16)


def dot(a, b, contract=((1,), (0,))):
    return lax.dot_general(a, b, (contract, ((), ())), preferred_element_type=F32)


def dot3(a, b, contract=((1,), (0,))):
    (a_high, a_low), (b_high, b_low) = a, b
    return (
        dot(a_high, b_high, contract) + dot(a_high, b_low, contract) + dot(a_low, b_high, contract)
    )


NT = ((1,), (1,))


def kernel(
    n_scen,
    n_col,
    quarter,
    sub,
    inv_hbm,
    coup_hbm,
    mask_ref,
    hess_ref,
    out_ref,
    flag_ref,
    inv,
    coup,
    high_t,
    low_t,
    prod,
    contrib,
    slots,
    corner_own,
    corner_slots,
    corner,
    scaled_high,
    scaled_low,
    y,
    y_next,
    y_high,
    y_low,
    solve_in,
    solve_out,
    back,
    load_sem,
    ring_send,
    ring_recv,
    sum_send,
    sum_recv,
    corner_send,
    corner_recv,
    fill_send,
    fill_recv,
    in_send,
    in_recv,
    back_send,
    back_recv,
):
    me = lax.axis_index("scen")
    z = lax.axis_index("col")
    depth = coup.shape[0]
    block = coup.shape[1]
    width = corner.shape[0]
    chunk = prod.shape[2]
    n_chunk = prod.shape[0]
    rows = block // n_scen
    piece = width // n_scen
    owners = width // rows
    tile = depth // mask_ref.shape[1]
    half = depth // 2
    n_sub = half // sub
    nb = width // 2

    barrier = pltpu.get_barrier_semaphore()

    coup_panel = pltpu.make_async_copy(
        coup_hbm.at[0, :, pl.ds(0, width)], coup.at[:, pl.ds(0, width)], load_sem.at[0]
    )
    coup_rest = pltpu.make_async_copy(
        coup_hbm.at[0, :, pl.ds(width, block - width)],
        coup.at[:, pl.ds(width, block - width)],
        load_sem.at[1],
    )
    inv_load = pltpu.make_async_copy(inv_hbm.at[0], inv, load_sem.at[2])
    coup_panel.start()

    @pl.when(z == 0)
    def _():
        inv_load.start()

    coup_rest.start()

    def greet_scen(k, _):
        pl.semaphore_signal(
            barrier,
            inc=1,
            device_id={"scen": lax.rem(me + k, n_scen)},
            device_id_type=pl.DeviceIdType.MESH,
        )
        return 0

    def greet_col(k, _):
        pl.semaphore_signal(
            barrier,
            inc=1,
            device_id={"col": lax.rem(z + k, n_col)},
            device_id_type=pl.DeviceIdType.MESH,
        )
        return 0

    lax.fori_loop(1, n_scen, greet_scen, 0)
    lax.fori_loop(1, n_col, greet_col, 0)
    pl.semaphore_wait(barrier, n_scen + n_col - 2)

    def ring_copy(q, way, s):
        at = prod.at[q, pl.ds(pl.multiple_of(way * half + s * sub, sub), sub), :]
        to = lax.rem(z + 1, n_col) if way == 0 else lax.rem(z + n_col - 1, n_col)
        return pltpu.make_async_remote_copy(
            src_ref=at,
            dst_ref=at,
            send_sem=ring_send.at[q, way, s],
            recv_sem=ring_recv.at[q, way, s],
            device_id={"col": to},
            device_id_type=pl.DeviceIdType.MESH,
        )

    def transpose_coupling(first, count):
        @pl.loop(0, depth // 128)
        def _(t):
            at = pl.ds(pl.multiple_of(t * 128, 128), 128)
            high, low = split(coup[at, pl.ds(first, count)].T)
            high_t[pl.ds(first, count), at] = high
            low_t[pl.ds(first, count), at] = low

    def contribute(q, first, count):
        p = split(prod[q])

        @pl.loop(0, count // quarter)
        def _(r):
            at = pl.ds(pl.multiple_of(first + r * quarter, quarter), quarter)
            contrib[q, at, :] = dot3((high_t[at, :], low_t[at, :]), p)

    def sum_copy(q, peer):
        slot = lax.rem(me - peer + n_scen, n_scen) - 1
        return pltpu.make_async_remote_copy(
            src_ref=contrib.at[q, pl.ds(pl.multiple_of(peer * rows, rows), rows), :],
            dst_ref=slots.at[q, slot],
            send_sem=sum_send.at[q],
            recv_sem=sum_recv.at[q],
            device_id={"scen": peer},
            device_id_type=pl.DeviceIdType.MESH,
        )

    def own_rows(q):
        own = contrib[q, pl.ds(pl.multiple_of(me * rows, rows), rows), :]
        return lax.fori_loop(0, n_scen - 1, lambda k, total: total + slots[q, k], own)

    def in_copy(slot):
        return pltpu.make_async_remote_copy(
            src_ref=solve_in.at[slot],
            dst_ref=solve_in.at[slot],
            send_sem=in_send,
            recv_sem=in_recv,
            device_id={"col": 0},
            device_id_type=pl.DeviceIdType.MESH,
        )

    def back_copy(to):
        return pltpu.make_async_remote_copy(
            src_ref=solve_out.at[to],
            dst_ref=back,
            send_sem=back_send,
            recv_sem=back_recv,
            device_id={"col": to},
            device_id_type=pl.DeviceIdType.MESH,
        )

    @pl.when(z == 0)
    def _():
        coup_panel.wait()
        transpose_coupling(0, width)
        inv_load.wait()
        keep = jnp.concatenate(
            [
                jnp.full((tile, 1), mask_ref[0, t], jnp.int32).astype(F32)
                for t in range(mask_ref.shape[1])
            ],
            axis=0,
        )

        for q in range(n_chunk):
            panel = split(coup[:, pl.ds(q * chunk, chunk)] * keep)
            for r in range(depth // quarter):
                n_half = half // quarter
                r = (r % 2) * n_half + r // 2
                kept = inv[pl.ds(r * quarter, quarter), :]
                scale = keep[r * quarter : (r + 1) * quarter]
                prod[q, pl.ds(r * quarter, quarter), :] = dot3(split(kept), panel) * scale
                way = r // n_half
                for s in range(quarter // sub):
                    ring_copy(q, way, (r % n_half) * (quarter // sub) + s).start()

        for q in range(n_chunk):
            p = split(prod[q])
            for r in range(width // quarter):
                at = pl.ds(r * quarter, quarter)
                corner_own[at, pl.ds(q * chunk, chunk)] = dot3((high_t[at, :], low_t[at, :]), p)

        def corner_start(k, _):
            peer = lax.rem(me + k, n_scen)
            pltpu.make_async_remote_copy(
                src_ref=corner_own.at[pl.ds(pl.multiple_of(peer * piece, piece), piece), :],
                dst_ref=corner_slots.at[n_scen - 1 - k],
                send_sem=corner_send,
                recv_sem=corner_recv,
                device_id={"scen": peer},
                device_id_type=pl.DeviceIdType.MESH,
            ).start()
            return 0

        lax.fori_loop(1, n_scen, corner_start, 0)

        coup_rest.wait()
        transpose_coupling(width, block - width)
        for q in range(n_chunk):
            contribute(q, width, block - width)

        mine = pl.ds(pl.multiple_of(me * piece, piece), piece)
        pltpu.make_async_copy(corner_slots, corner_slots, corner_recv).wait()
        total = lax.fori_loop(
            0, n_scen - 1, lambda k, total: total + corner_slots[k], corner_own[mine, :]
        )
        row = me * piece + lax.broadcasted_iota(jnp.int32, (piece, width), 0)
        column = lax.broadcasted_iota(jnp.int32, (piece, width), 1)
        corner[mine, :] = total + jnp.where(row == column, hess_ref[...], 0.0)

        def fill_copy(k):
            return pltpu.make_async_remote_copy(
                src_ref=corner.at[mine, :],
                dst_ref=corner.at[mine, :],
                send_sem=fill_send,
                recv_sem=fill_recv.at[n_scen - 1 - k],
                device_id={"scen": lax.rem(me + k, n_scen)},
                device_id_type=pl.DeviceIdType.MESH,
            )

        def fill_start(k, _):
            fill_copy(k).start()
            return 0

        lax.fori_loop(1, n_scen, fill_start, 0)

        def sum_start(k, _):
            peer = lax.rem(me + k, n_scen)

            @pl.when(peer >= owners)
            def _():
                for q in range(n_chunk):
                    sum_copy(q, peer).start()

            return 0

        lax.fori_loop(1, n_scen, sum_start, 0)

        def fill_wait(k, _):
            from_peer = lax.rem(me + k, n_scen)
            theirs = corner.at[pl.ds(pl.multiple_of(from_peer * piece, piece), piece), :]
            pltpu.make_async_copy(theirs, theirs, fill_recv.at[k - 1]).wait()
            return 0

        lax.fori_loop(1, n_scen, fill_wait, 0)

        row = lax.broadcasted_iota(jnp.int32, (width, width), 0)
        column = lax.broadcasted_iota(jnp.int32, (width, width), 1)
        on_diagonal = jnp.where(row == column, corner[...], 0.0)
        root_row = lax.rsqrt(jnp.sum(on_diagonal, axis=0, keepdims=True))
        root_column = lax.rsqrt(jnp.sum(on_diagonal, axis=1, keepdims=True))
        scaled = corner[...] * root_column * root_row
        high, low = split(scaled)
        scaled_high[...] = high
        scaled_low[...] = low
        y[...] = jnp.where(row == column, 1.0, jnp.where(row > column, -scaled, 0.0))

        for step in range(STEPS):
            high, low = split(y[...])
            y_high[...] = high
            y_low[...] = low
            size = jnp.zeros((1, 1), F32)
            for r in range(2):
                at = pl.ds(r * nb, nb)
                to = pl.ds(0, (r + 1) * nb)
                t = dot3((y_high[at, to], y_low[at, to]), (scaled_high[to, to], scaled_low[to, to]))
                e = dot3(split(t), (y_high[to, to], y_low[to, to]), NT)
                e_row = r * nb + lax.broadcasted_iota(jnp.int32, e.shape, 0)
                e_column = lax.broadcasted_iota(jnp.int32, e.shape, 1)
                e = jnp.where(e_row == e_column, e - 1.0, jnp.where(e_row > e_column, e, 0.0))
                if step == STEPS - 1:
                    size = size + jnp.sum(e * e, keepdims=True)
                e = jnp.where(e_row == e_column, 0.5 * e, e)
                y_next[at, to] = y[at, to] - dot3(split(e), (y_high[to, to], y_low[to, to]))
            for r in range(2):
                at = pl.ds(r * nb, nb)
                to = pl.ds(0, (r + 1) * nb)
                y[at, to] = y_next[at, to]

        bad = jnp.where(size < SETTLED, 0.0, 1.0)
        y_final = split(y[...])

        @pl.when(me < owners)
        def _():
            solve_in[0] = corner[
                pl.ds(pl.multiple_of(lax.rem(me, owners) * rows, rows), rows), :
            ]

        @pl.when(me >= owners)
        def _():
            for q in range(n_chunk):
                pltpu.make_async_copy(slots.at[q], slots.at[q], sum_recv.at[q]).wait()
                solve_in[0, :, pl.ds(q * chunk, chunk)] = own_rows(q)

        rest = solve_in.at[pl.ds(1, n_col - 1)]
        pltpu.make_async_copy(rest, rest, in_recv).wait()
        given = solve_in[...].reshape(n_col * rows, width) * root_row
        solved = dot3(split(given), y_final, NT).reshape(n_col, rows, width)
        solve_out[:, pl.ds(0, rows), :] = solved
        solve_out[:, pl.ds(rows, 8), :] = jnp.broadcast_to(bad, (n_col, 8, width))

        def back_start(k, _):
            back_copy(k).start()
            return 0

        lax.fori_loop(1, n_col, back_start, 0)
        row = me * rows + lax.broadcasted_iota(jnp.int32, (rows, width), 0)
        column = lax.broadcasted_iota(jnp.int32, (rows, width), 1)
        out_ref[...] = jnp.where(column <= row, solved[0], 0.0)
        flag_ref[...] = jnp.broadcast_to(bad, flag_ref.shape)

        for q in range(n_chunk):
            for way in range(2):
                for s in range(n_sub):
                    ring_copy(q, way, s).wait_send()
        pltpu.make_async_copy(corner_slots, corner_slots, corner_send).wait()
        pltpu.make_async_copy(corner_slots, corner_slots, fill_send).wait()
        for q in range(n_chunk):

            @pl.when(me < owners)
            def _():
                some = slots.at[q, pl.ds(0, n_scen - owners)]
                pltpu.make_async_copy(some, some, sum_send.at[q]).wait()

            @pl.when(me >= owners)
            def _():
                some = slots.at[q, pl.ds(0, n_scen - owners - 1)]
                pltpu.make_async_copy(some, some, sum_send.at[q]).wait()

        some = solve_out.at[pl.ds(1, n_col - 1)]
        pltpu.make_async_copy(some, some, back_send).wait()

    @pl.when(z != 0)
    def _():
        coup_panel.wait()
        coup_rest.wait()
        transpose_coupling(0, block)

        def sum_start(q):
            def start(k, _):
                sum_copy(q, lax.rem(me + k, n_scen)).start()
                return 0

            lax.fori_loop(1, n_scen, start, 0)

        for q in range(n_chunk):

            @pl.loop(0, n_sub)
            def _(s):
                up = ring_copy(q, 0, s)
                up.wait_recv()

                @pl.when(z < n_col - 1)
                def _():
                    up.start()

                down = ring_copy(q, 1, s)
                down.wait_recv()

                @pl.when(z > 1)
                def _():
                    down.start()

            contribute(q, 0, block)
            sum_start(q)

        for q in range(n_chunk):
            pltpu.make_async_copy(slots.at[q], slots.at[q], sum_recv.at[q]).wait()
            solve_in[z, :, pl.ds(q * chunk, chunk)] = own_rows(q)
        in_copy(z).start()

        for q in range(n_chunk):

            @pl.loop(0, n_sub)
            def _(s):
                @pl.when(z < n_col - 1)
                def _():
                    ring_copy(q, 0, s).wait_send()

                @pl.when(z > 1)
                def _():
                    ring_copy(q, 1, s).wait_send()

            pltpu.make_async_copy(slots.at[q], slots.at[q], sum_send.at[q]).wait()
        in_copy(z).wait_send()
        pltpu.make_async_copy(back, back, back_recv).wait()
        out_ref[...] = back[pl.ds(0, rows), :]
        flag_ref[...] = back[pl.ds(rows, 8), pl.ds(0, 128)]


def fused(inverses, coupling, tile_mask, hess_diag, quarter=256, chunk=256, sub=64):
    n_scen = lax.axis_size("scen")
    n_col = lax.axis_size("col")
    _, depth, block = coupling.shape
    width = hess_diag.shape[0]
    rows = block // n_scen
    piece = width // n_scen
    n_chunk = width // chunk
    n_sub = depth // 2 // sub
    vmem = pltpu.VMEM
    dma = pltpu.SemaphoreType.DMA
    scratch = [
        vmem((depth, depth), F32),
        vmem((depth, block), F32),
        vmem((block, depth), BF16),
        vmem((block, depth), BF16),
        vmem((n_chunk, depth, chunk), F32),
        vmem((n_chunk, block, chunk), F32),
        vmem((n_chunk, n_scen - 1, rows, chunk), F32),
        vmem((width, width), F32),
        vmem((n_scen - 1, piece, width), F32),
        vmem((width, width), F32),
        vmem((width, width), BF16),
        vmem((width, width), BF16),
        vmem((width, width), F32),
        vmem((width, width), F32),
        vmem((width, width), BF16),
        vmem((width, width), BF16),
        vmem((n_col, rows, width), F32),
        vmem((n_col, rows + 8, width), F32),
        vmem((rows + 8, width), F32),
        dma((3,)),
        dma((n_chunk, 2, n_sub)),
        dma((n_chunk, 2, n_sub)),
        dma((n_chunk,)),
        dma((n_chunk,)),
        dma(()),
        dma(()),
        dma(()),
        dma((n_scen - 1,)),
        dma(()),
        dma(()),
        dma(()),
        dma(()),
    ]
    return pl.pallas_call(
        functools.partial(kernel, n_scen, n_col, quarter, sub),
        out_shape=(
            jax.ShapeDtypeStruct((rows, width), F32),
            jax.ShapeDtypeStruct((8, 128), F32),
        ),
        in_specs=[
            pl.BlockSpec(memory_space=pl.ANY),
            pl.BlockSpec(memory_space=pl.ANY),
            pl.BlockSpec(memory_space=pltpu.SMEM),
            pl.BlockSpec(memory_space=pltpu.VMEM),
        ],
        out_specs=[pl.BlockSpec(memory_space=pltpu.VMEM)] * 2,
        scratch_shapes=scratch,
        compiler_params=pltpu.CompilerParams(
            collective_id=0, has_side_effects=True, vmem_limit_bytes=50 * 2**20
        ),
    )(inverses, coupling, tile_mask, hess_diag[None, :])


def body(inverses, coupling, tile_mask, hess_diag):
    factor, flag = fused(inverses, coupling, tile_mask, hess_diag)
    return lax.cond(
        flag[0, 0] > 0.5,
        direct_body,
        lambda *_: factor,
        inverses,
        coupling,
        tile_mask,
        hess_diag,
    )


def solution(mesh):
    in_specs = (P("scen", None, None), P("scen", None, "col"), P("scen", None), P())
    out_specs = P(("col", "scen"), None)
    return jax.shard_map(body, mesh=mesh, in_specs=in_specs, out_specs=out_specs, check_vma=False)
```

```python
import functools

import jax
import jax.numpy as jnp
from jax import lax
from jax.experimental import pallas as pl
from jax.experimental.pallas import tpu as pltpu
from jax.sharding import PartitionSpec as P


def filled_up(lines, size):
    spare = -lines.shape[0] % size
    if not spare:
        return lines
    return jnp.concatenate([lines, jnp.zeros((spare, *lines.shape[1:]), lines.dtype)])


def spread(x, axis, root):
    lines = jnp.where(lax.axis_index(axis) == root, x, jnp.zeros_like(x)).reshape(
        -1, *x.shape[1:][-1:]
    )
    padded = filled_up(lines, lax.axis_size(axis))
    own = lax.psum_scatter(padded, axis, scatter_dimension=0, tiled=True)
    return lax.all_gather(own, axis, axis=0, tiled=True)[: len(lines)].reshape(x.shape)


def in_blocks(x, dim, size):
    lengths = x.shape
    blocks = x.reshape(*lengths[:dim], size, lengths[dim] // size, *lengths[dim + 1 :])
    return jnp.moveaxis(blocks, dim, 0)


def sum_at_owner(x, axis, dim):
    size = lax.axis_size(axis)
    blocks = lax.all_to_all(in_blocks(x, dim, size), axis, 0, 0, tiled=True)
    return jnp.sum(blocks, axis=0)


def sent_to_all(x, axis):
    size = lax.axis_size(axis)
    return lax.all_to_all(jnp.broadcast_to(x[None], (size, *x.shape)), axis, 0, 0, tiled=True)


def in_order(blocks, dim):
    lengths = list(blocks.shape[1:])
    lengths[dim] *= blocks.shape[0]
    return jnp.moveaxis(blocks, 0, dim).reshape(lengths)


def collect(x, axis, dim):
    blocks = sent_to_all(x, axis)
    return in_order(blocks, dim)


def from_root(x, axis, root):
    return lax.dynamic_index_in_dim(lax.all_gather(x, axis), root, 0, keepdims=False)


def outer_rows(left, piece):
    return lax.dot_general(
        left,
        piece,
        (((0,), (0,)), ((), ())),
        precision=lax.Precision.HIGHEST,
        preferred_element_type=jnp.float32,
    )


def matmul(left, right):
    return jnp.dot(left, right, precision=lax.Precision.HIGHEST, preferred_element_type=jnp.float32)


def direct_body(inverses, coupling, tile_mask, hess_diag):
    inverse = inverses[0]
    local = coupling[0]
    width = hess_diag.shape[0]
    half = width // 2
    scen_size = lax.axis_size("scen")
    rows = local.shape[1] // scen_size
    row_keep = jnp.repeat(tile_mask[0].astype(jnp.float32), local.shape[0] // tile_mask.shape[1])
    panel = spread(local[:, :width], "col", 0)
    panel = panel * row_keep[:, None]
    product = matmul(inverse, panel) * row_keep[:, None]
    block = local
    summed = sum_at_owner(outer_rows(block, product), "scen", 0)
    first = lax.axis_index("col") * local.shape[1] + lax.axis_index("scen") * rows
    global_rows = first + jnp.arange(rows, dtype=jnp.int32)
    columns = jnp.arange(width, dtype=jnp.int32)
    schur = summed + jnp.where(columns[None, :] == global_rows[:, None], hess_diag[None, :], 0.0)

    def fetch(stacked, low):
        whole = collect(stacked, "scen", 1)
        block = whole[:, low : low + half]
        return from_root(block, "col", 0)

    identity = jnp.eye(half, dtype=jnp.float32)
    block_one = fetch(schur[None, :, :half], 0)[0]
    chol1 = jnp.linalg.cholesky(block_one)
    inv1 = jax.scipy.linalg.solve_triangular(chol1, identity, lower=True)
    lcol1 = matmul(schur[:, :half], inv1.T)
    own_one = lax.dynamic_slice_in_dim(chol1, jnp.clip(first, 0, half - rows), rows, 0)
    lcol1 = jnp.where(first < half, own_one, lcol1)
    paired = fetch(jnp.stack([schur[:, half:], lcol1]), half)
    lower_b = paired[1]
    update = paired[0] - matmul(lower_b, lower_b.T)
    chol2 = jnp.linalg.cholesky(update)
    inv2 = jax.scipy.linalg.solve_triangular(chol2, identity, lower=True)
    remain = schur[:, half:] - matmul(lcol1, lower_b.T)
    lcol2 = matmul(remain, inv2.T)
    own_two = lax.dynamic_slice_in_dim(chol2, jnp.clip(first - half, 0, half - rows), rows, 0)
    lcol2 = jnp.where(first < width, own_two, lcol2)
    lcol2 = jnp.where(first < half, jnp.zeros_like(lcol2), lcol2)
    return jnp.concatenate([lcol1, lcol2], axis=1)


F32 = jnp.float32
BF16 = jnp.bfloat16
STEPS = 3
SETTLED = 1.6e-5


def split(x):
    high = x.astype(BF16)
    return high, (x - high.astype(F32)).astype(BF16)


def dot(a, b, contract=((1,), (0,))):
    return lax.dot_general(a, b, (contract, ((), ())), preferred_element_type=F32)


def dot3(a, b, contract=((1,), (0,))):
    (a_high, a_low), (b_high, b_low) = a, b
    return (
        dot(a_high, b_high, contract) + dot(a_high, b_low, contract) + dot(a_low, b_high, contract)
    )


NT = ((1,), (1,))


def kernel(
    n_scen,
    n_col,
    quarter,
    sub,
    inv_hbm,
    coup_hbm,
    mask_ref,
    hess_ref,
    out_ref,
    flag_ref,
    inv,
    coup,
    high_t,
    low_t,
    prod,
    prod_high,
    prod_low,
    contrib,
    slots,
    corner_own,
    corner_slots,
    corner,
    scaled_high,
    scaled_low,
    y,
    y_next,
    y_high,
    y_low,
    solve_in,
    solve_out,
    back,
    load_sem,
    ring_send,
    ring_recv,
    sum_send,
    sum_recv,
    corner_send,
    corner_recv,
    fill_send,
    fill_recv,
    in_send,
    in_recv,
    back_send,
    back_recv,
):
    me = lax.axis_index("scen")
    z = lax.axis_index("col")
    depth = coup.shape[0]
    block = coup.shape[1]
    width = corner.shape[0]
    chunk = prod.shape[2]
    n_chunk = prod.shape[0]
    rows = block // n_scen
    piece = width // n_scen
    owners = width // rows
    tile = depth // mask_ref.shape[1]
    half = depth // 2
    n_sub = half // sub
    nb = width // 2

    barrier = pltpu.get_barrier_semaphore()

    coup_panel = pltpu.make_async_copy(
        coup_hbm.at[0, :, pl.ds(0, width)], coup.at[:, pl.ds(0, width)], load_sem.at[0]
    )
    coup_rest = pltpu.make_async_copy(
        coup_hbm.at[0, :, pl.ds(width, block - width)],
        coup.at[:, pl.ds(width, block - width)],
        load_sem.at[1],
    )
    inv_load = pltpu.make_async_copy(inv_hbm.at[0], inv, load_sem.at[2])
    coup_panel.start()

    @pl.when(z == 0)
    def _():
        inv_load.start()

    coup_rest.start()

    def greet_scen(k, _):
        pl.semaphore_signal(
            barrier,
            inc=1,
            device_id={"scen": lax.rem(me + k, n_scen)},
            device_id_type=pl.DeviceIdType.MESH,
        )
        return 0

    def greet_col(k, _):
        pl.semaphore_signal(
            barrier,
            inc=1,
            device_id={"col": lax.rem(z + k, n_col)},
            device_id_type=pl.DeviceIdType.MESH,
        )
        return 0

    lax.fori_loop(1, n_scen, greet_scen, 0)
    lax.fori_loop(1, n_col, greet_col, 0)
    pl.semaphore_wait(barrier, n_scen + n_col - 2)

    def ring_copy(way, g):
        s = lax.rem(g, n_sub)
        at = prod.at[g // n_sub, pl.ds(pl.multiple_of(way * half + s * sub, sub), sub), :]
        to = lax.rem(z + 1, n_col) if way == 0 else lax.rem(z + n_col - 1, n_col)
        return pltpu.make_async_remote_copy(
            src_ref=at,
            dst_ref=at,
            send_sem=ring_send.at[way, g],
            recv_sem=ring_recv.at[way, g],
            device_id={"col": to},
            device_id_type=pl.DeviceIdType.MESH,
        )

    def transpose_coupling(first, count):
        @pl.loop(0, depth // 128)
        def _(t):
            at = pl.ds(pl.multiple_of(t * 128, 128), 128)
            high, low = split(coup[at, pl.ds(first, count)].T)
            high_t[pl.ds(first, count), at] = high
            low_t[pl.ds(first, count), at] = low

    def split_prod(q):
        high, low = split(prod[q])
        prod_high[...] = high
        prod_low[...] = low

    def contribute(q, first):
        at = pl.ds(pl.multiple_of(first, quarter), quarter)
        contrib[q, at, :] = dot3(
            (high_t[at, :], low_t[at, :]), (prod_high[...], prod_low[...])
        )

    def sum_copy(q, peer):
        slot = lax.rem(me - peer + n_scen, n_scen) - 1
        return pltpu.make_async_remote_copy(
            src_ref=contrib.at[q, pl.ds(pl.multiple_of(peer * rows, rows), rows), :],
            dst_ref=slots.at[q, slot],
            send_sem=sum_send.at[q],
            recv_sem=sum_recv.at[q],
            device_id={"scen": peer},
            device_id_type=pl.DeviceIdType.MESH,
        )

    def own_rows(q):
        own = contrib[q, pl.ds(pl.multiple_of(me * rows, rows), rows), :]
        return lax.fori_loop(0, n_scen - 1, lambda k, total: total + slots[q, k], own)

    def in_copy(slot):
        return pltpu.make_async_remote_copy(
            src_ref=solve_in.at[slot],
            dst_ref=solve_in.at[slot],
            send_sem=in_send,
            recv_sem=in_recv,
            device_id={"col": 0},
            device_id_type=pl.DeviceIdType.MESH,
        )

    def back_copy(to):
        return pltpu.make_async_remote_copy(
            src_ref=solve_out.at[to],
            dst_ref=back,
            send_sem=back_send,
            recv_sem=back_recv,
            device_id={"col": to},
            device_id_type=pl.DeviceIdType.MESH,
        )

    @pl.when(z == 0)
    def _():
        coup_panel.wait()
        transpose_coupling(0, width)
        inv_load.wait()
        keep = jnp.concatenate(
            [
                jnp.full((tile, 1), mask_ref[0, t], jnp.int32).astype(F32)
                for t in range(mask_ref.shape[1])
            ],
            axis=0,
        )

        for q in range(n_chunk):
            panel = split(coup[:, pl.ds(q * chunk, chunk)] * keep)
            for r in range(depth // quarter):
                n_half = half // quarter
                r = (r % 2) * n_half + r // 2
                kept = inv[pl.ds(r * quarter, quarter), :]
                scale = keep[r * quarter : (r + 1) * quarter]
                prod[q, pl.ds(r * quarter, quarter), :] = dot3(split(kept), panel) * scale
                way = r // n_half
                for s in range(quarter // sub):
                    ring_copy(way, q * n_sub + (r % n_half) * (quarter // sub) + s).start()

        for q in range(n_chunk):
            p = split(prod[q])
            for r in range(width // quarter):
                at = pl.ds(r * quarter, quarter)
                corner_own[at, pl.ds(q * chunk, chunk)] = dot3((high_t[at, :], low_t[at, :]), p)

        def corner_start(k, _):
            peer = lax.rem(me + k, n_scen)
            pltpu.make_async_remote_copy(
                src_ref=corner_own.at[pl.ds(pl.multiple_of(peer * piece, piece), piece), :],
                dst_ref=corner_slots.at[n_scen - 1 - k],
                send_sem=corner_send,
                recv_sem=corner_recv,
                device_id={"scen": peer},
                device_id_type=pl.DeviceIdType.MESH,
            ).start()
            return 0

        lax.fori_loop(1, n_scen, corner_start, 0)

        coup_rest.wait()
        transpose_coupling(width, block - width)
        for q in range(n_chunk):
            split_prod(q)

            @pl.loop(width // quarter, block // quarter)
            def _(r):
                contribute(q, r * quarter)


        mine = pl.ds(pl.multiple_of(me * piece, piece), piece)
        pltpu.make_async_copy(corner_slots, corner_slots, corner_recv).wait()
        total = lax.fori_loop(
            0, n_scen - 1, lambda k, total: total + corner_slots[k], corner_own[mine, :]
        )
        row = me * piece + lax.broadcasted_iota(jnp.int32, (piece, width), 0)
        column = lax.broadcasted_iota(jnp.int32, (piece, width), 1)
        corner[mine, :] = total + jnp.where(row == column, hess_ref[...], 0.0)

        def fill_copy(k):
            return pltpu.make_async_remote_copy(
                src_ref=corner.at[mine, :],
                dst_ref=corner.at[mine, :],
                send_sem=fill_send,
                recv_sem=fill_recv.at[n_scen - 1 - k],
                device_id={"scen": lax.rem(me + k, n_scen)},
                device_id_type=pl.DeviceIdType.MESH,
            )

        def fill_start(k, _):
            fill_copy(k).start()
            return 0

        lax.fori_loop(1, n_scen, fill_start, 0)

        def sum_start(k, _):
            peer = lax.rem(me + k, n_scen)

            @pl.when(peer >= owners)
            def _():
                for q in range(n_chunk):
                    sum_copy(q, peer).start()

            return 0

        lax.fori_loop(1, n_scen, sum_start, 0)

        def fill_wait(k, _):
            from_peer = lax.rem(me + k, n_scen)
            theirs = corner.at[pl.ds(pl.multiple_of(from_peer * piece, piece), piece), :]
            pltpu.make_async_copy(theirs, theirs, fill_recv.at[k - 1]).wait()
            return 0

        lax.fori_loop(1, n_scen, fill_wait, 0)

        row = lax.broadcasted_iota(jnp.int32, (width, width), 0)
        column = lax.broadcasted_iota(jnp.int32, (width, width), 1)
        on_diagonal = jnp.where(row == column, corner[...], 0.0)
        root_row = lax.rsqrt(jnp.sum(on_diagonal, axis=0, keepdims=True))
        root_column = lax.rsqrt(jnp.sum(on_diagonal, axis=1, keepdims=True))
        scaled = corner[...] * root_column * root_row
        high, low = split(scaled)
        scaled_high[...] = high
        scaled_low[...] = low
        y[...] = jnp.where(row == column, 1.0, jnp.where(row > column, -scaled, 0.0))

        for step in range(STEPS):
            high, low = split(y[...])
            y_high[...] = high
            y_low[...] = low
            size = jnp.zeros((1, 1), F32)
            for r in range(2):
                at = pl.ds(r * nb, nb)
                to = pl.ds(0, (r + 1) * nb)
                t = dot3((y_high[at, to], y_low[at, to]), (scaled_high[to, to], scaled_low[to, to]))
                e = dot3(split(t), (y_high[to, to], y_low[to, to]), NT)
                e_row = r * nb + lax.broadcasted_iota(jnp.int32, e.shape, 0)
                e_column = lax.broadcasted_iota(jnp.int32, e.shape, 1)
                e = jnp.where(e_row == e_column, e - 1.0, jnp.where(e_row > e_column, e, 0.0))
                if step == STEPS - 1:
                    size = size + jnp.sum(e * e, keepdims=True)
                e = jnp.where(e_row == e_column, 0.5 * e, e)
                y_next[at, to] = y[at, to] - dot3(split(e), (y_high[to, to], y_low[to, to]))
            for r in range(2):
                at = pl.ds(r * nb, nb)
                to = pl.ds(0, (r + 1) * nb)
                y[at, to] = y_next[at, to]

        bad = jnp.where(size < SETTLED, 0.0, 1.0)
        y_final = split(y[...])

        @pl.when(me < owners)
        def _():
            solve_in[0] = corner[
                pl.ds(pl.multiple_of(lax.rem(me, owners) * rows, rows), rows), :
            ]

        @pl.when(me >= owners)
        def _():
            for q in range(n_chunk):
                pltpu.make_async_copy(slots.at[q], slots.at[q], sum_recv.at[q]).wait()
                solve_in[0, :, pl.ds(q * chunk, chunk)] = own_rows(q)

        rest = solve_in.at[pl.ds(1, n_col - 1)]
        pltpu.make_async_copy(rest, rest, in_recv).wait()
        given = solve_in[...].reshape(n_col * rows, width) * root_row
        solved = dot3(split(given), y_final, NT).reshape(n_col, rows, width)
        solve_out[:, pl.ds(0, rows), :] = solved
        solve_out[:, pl.ds(rows, 8), :] = jnp.broadcast_to(bad, (n_col, 8, width))

        def back_start(k, _):
            back_copy(k).start()
            return 0

        lax.fori_loop(1, n_col, back_start, 0)
        row = me * rows + lax.broadcasted_iota(jnp.int32, (rows, width), 0)
        column = lax.broadcasted_iota(jnp.int32, (rows, width), 1)
        out_ref[...] = jnp.where(column <= row, solved[0], 0.0)
        flag_ref[...] = jnp.broadcast_to(bad, flag_ref.shape)

        @pl.loop(0, n_chunk * n_sub)
        def _(g):
            ring_copy(0, g).wait_send()
            ring_copy(1, g).wait_send()

        pltpu.make_async_copy(corner_slots, corner_slots, corner_send).wait()
        pltpu.make_async_copy(corner_slots, corner_slots, fill_send).wait()
        for q in range(n_chunk):

            @pl.when(me < owners)
            def _():
                some = slots.at[q, pl.ds(0, n_scen - owners)]
                pltpu.make_async_copy(some, some, sum_send.at[q]).wait()

            @pl.when(me >= owners)
            def _():
                some = slots.at[q, pl.ds(0, n_scen - owners - 1)]
                pltpu.make_async_copy(some, some, sum_send.at[q]).wait()

        some = solve_out.at[pl.ds(1, n_col - 1)]
        pltpu.make_async_copy(some, some, back_send).wait()

    @pl.when(z != 0)
    def _():
        coup_panel.wait()
        coup_rest.wait()
        transpose_coupling(0, block)

        def form(q, r):
            contribute(q, r * quarter)
            per = quarter // rows

            def start(k, _):
                peer = lax.rem(me + k, per) + r * per

                @pl.when(peer != me)
                def _():
                    sum_copy(q, peer).start()

                return 0

            lax.fori_loop(0, per, start, 0)

        late = jnp.maximum(z - 1, n_col - 1 - z)
        n_piece = n_chunk * n_sub
        n_row = block // quarter

        @pl.loop(0, n_piece + late)
        def _(t):
            g = t - (z - 1)

            @pl.when(jnp.logical_and(g >= 0, g < n_piece))
            def _():
                up = ring_copy(0, g)
                up.wait_recv()

                @pl.when(z < n_col - 1)
                def _():
                    up.start()

            h = t - (n_col - 1 - z)

            @pl.when(jnp.logical_and(h >= 0, h < n_piece))
            def _():
                down = ring_copy(1, h)
                down.wait_recv()

                @pl.when(z > 1)
                def _():
                    down.start()

            done = t - late + 1
            q = done // n_sub - 1
            r = lax.rem(done, n_sub)
            whole = done >= n_sub

            @pl.when(jnp.logical_and(whole, r == 0))
            def _():
                split_prod(q)

            @pl.when(jnp.logical_and(jnp.logical_and(whole, r < n_row), done < n_piece))
            def _():
                form(q, r)

        @pl.loop(0, n_row)
        def _(r):
            form(n_chunk - 1, r)

        for q in range(n_chunk):
            pltpu.make_async_copy(slots.at[q], slots.at[q], sum_recv.at[q]).wait()
            solve_in[z, :, pl.ds(q * chunk, chunk)] = own_rows(q)
        in_copy(z).start()

        for q in range(n_chunk):

            pltpu.make_async_copy(slots.at[q], slots.at[q], sum_send.at[q]).wait()
        in_copy(z).wait_send()

        @pl.loop(0, n_piece)
        def _(g):
            @pl.when(z < n_col - 1)
            def _():
                ring_copy(0, g).wait_send()

            @pl.when(z > 1)
            def _():
                ring_copy(1, g).wait_send()

        pltpu.make_async_copy(back, back, back_recv).wait()
        out_ref[...] = back[pl.ds(0, rows), :]
        flag_ref[...] = back[pl.ds(rows, 8), pl.ds(0, 128)]


def fused(inverses, coupling, tile_mask, hess_diag, quarter=256, chunk=256, sub=128):
    n_scen = lax.axis_size("scen")
    n_col = lax.axis_size("col")
    _, depth, block = coupling.shape
    width = hess_diag.shape[0]
    rows = block // n_scen
    piece = width // n_scen
    n_chunk = width // chunk
    n_sub = depth // 2 // sub
    vmem = pltpu.VMEM
    dma = pltpu.SemaphoreType.DMA
    scratch = [
        vmem((depth, depth), F32),
        vmem((depth, block), F32),
        vmem((block, depth), BF16),
        vmem((block, depth), BF16),
        vmem((n_chunk, depth, chunk), F32),
        vmem((depth, chunk), BF16),
        vmem((depth, chunk), BF16),
        vmem((n_chunk, block, chunk), F32),
        vmem((n_chunk, n_scen - 1, rows, chunk), F32),
        vmem((width, width), F32),
        vmem((n_scen - 1, piece, width), F32),
        vmem((width, width), F32),
        vmem((width, width), BF16),
        vmem((width, width), BF16),
        vmem((width, width), F32),
        vmem((width, width), F32),
        vmem((width, width), BF16),
        vmem((width, width), BF16),
        vmem((n_col, rows, width), F32),
        vmem((n_col, rows + 8, width), F32),
        vmem((rows + 8, width), F32),
        dma((3,)),
        dma((2, n_chunk * n_sub)),
        dma((2, n_chunk * n_sub)),
        dma((n_chunk,)),
        dma((n_chunk,)),
        dma(()),
        dma(()),
        dma(()),
        dma((n_scen - 1,)),
        dma(()),
        dma(()),
        dma(()),
        dma(()),
    ]
    return pl.pallas_call(
        functools.partial(kernel, n_scen, n_col, quarter, sub),
        out_shape=(
            jax.ShapeDtypeStruct((rows, width), F32),
            jax.ShapeDtypeStruct((8, 128), F32),
        ),
        in_specs=[
            pl.BlockSpec(memory_space=pl.ANY),
            pl.BlockSpec(memory_space=pl.ANY),
            pl.BlockSpec(memory_space=pltpu.SMEM),
            pl.BlockSpec(memory_space=pltpu.VMEM),
        ],
        out_specs=[pl.BlockSpec(memory_space=pltpu.VMEM)] * 2,
        scratch_shapes=scratch,
        compiler_params=pltpu.CompilerParams(
            collective_id=0, has_side_effects=True, vmem_limit_bytes=50 * 2**20
        ),
    )(inverses, coupling, tile_mask, hess_diag[None, :])


def body(inverses, coupling, tile_mask, hess_diag):
    factor, flag = fused(inverses, coupling, tile_mask, hess_diag)
    return lax.cond(
        flag[0, 0] > 0.5,
        direct_body,
        lambda *_: factor,
        inverses,
        coupling,
        tile_mask,
        hess_diag,
    )


def solution(mesh):
    in_specs = (P("scen", None, None), P("scen", None, "col"), P("scen", None), P())
    out_specs = P(("col", "scen"), None)
    return jax.shard_map(body, mesh=mesh, in_specs=in_specs, out_specs=out_specs, check_vma=False)
```

```python
import functools

import jax
import jax.numpy as jnp
from jax import lax
from jax.experimental import pallas as pl
from jax.experimental.pallas import tpu as pltpu
from jax.sharding import PartitionSpec as P


def filled_up(lines, size):
    spare = -lines.shape[0] % size
    if not spare:
        return lines
    return jnp.concatenate([lines, jnp.zeros((spare, *lines.shape[1:]), lines.dtype)])


def spread(x, axis, root):
    lines = jnp.where(lax.axis_index(axis) == root, x, jnp.zeros_like(x)).reshape(
        -1, *x.shape[1:][-1:]
    )
    padded = filled_up(lines, lax.axis_size(axis))
    own = lax.psum_scatter(padded, axis, scatter_dimension=0, tiled=True)
    return lax.all_gather(own, axis, axis=0, tiled=True)[: len(lines)].reshape(x.shape)


def in_blocks(x, dim, size):
    lengths = x.shape
    blocks = x.reshape(*lengths[:dim], size, lengths[dim] // size, *lengths[dim + 1 :])
    return jnp.moveaxis(blocks, dim, 0)


def sum_at_owner(x, axis, dim):
    size = lax.axis_size(axis)
    blocks = lax.all_to_all(in_blocks(x, dim, size), axis, 0, 0, tiled=True)
    return jnp.sum(blocks, axis=0)


def sent_to_all(x, axis):
    size = lax.axis_size(axis)
    return lax.all_to_all(jnp.broadcast_to(x[None], (size, *x.shape)), axis, 0, 0, tiled=True)


def in_order(blocks, dim):
    lengths = list(blocks.shape[1:])
    lengths[dim] *= blocks.shape[0]
    return jnp.moveaxis(blocks, 0, dim).reshape(lengths)


def collect(x, axis, dim):
    blocks = sent_to_all(x, axis)
    return in_order(blocks, dim)


def from_root(x, axis, root):
    return lax.dynamic_index_in_dim(lax.all_gather(x, axis), root, 0, keepdims=False)


def outer_rows(left, piece):
    return lax.dot_general(
        left,
        piece,
        (((0,), (0,)), ((), ())),
        precision=lax.Precision.HIGHEST,
        preferred_element_type=jnp.float32,
    )


def matmul(left, right):
    return jnp.dot(left, right, precision=lax.Precision.HIGHEST, preferred_element_type=jnp.float32)


def direct_body(inverses, coupling, tile_mask, hess_diag):
    inverse = inverses[0]
    local = coupling[0]
    width = hess_diag.shape[0]
    half = width // 2
    scen_size = lax.axis_size("scen")
    rows = local.shape[1] // scen_size
    row_keep = jnp.repeat(tile_mask[0].astype(jnp.float32), local.shape[0] // tile_mask.shape[1])
    panel = spread(local[:, :width], "col", 0)
    panel = panel * row_keep[:, None]
    product = matmul(inverse, panel) * row_keep[:, None]
    block = local
    summed = sum_at_owner(outer_rows(block, product), "scen", 0)
    first = lax.axis_index("col") * local.shape[1] + lax.axis_index("scen") * rows
    global_rows = first + jnp.arange(rows, dtype=jnp.int32)
    columns = jnp.arange(width, dtype=jnp.int32)
    schur = summed + jnp.where(columns[None, :] == global_rows[:, None], hess_diag[None, :], 0.0)

    def fetch(stacked, low):
        whole = collect(stacked, "scen", 1)
        block = whole[:, low : low + half]
        return from_root(block, "col", 0)

    identity = jnp.eye(half, dtype=jnp.float32)
    block_one = fetch(schur[None, :, :half], 0)[0]
    chol1 = jnp.linalg.cholesky(block_one)
    inv1 = jax.scipy.linalg.solve_triangular(chol1, identity, lower=True)
    lcol1 = matmul(schur[:, :half], inv1.T)
    own_one = lax.dynamic_slice_in_dim(chol1, jnp.clip(first, 0, half - rows), rows, 0)
    lcol1 = jnp.where(first < half, own_one, lcol1)
    paired = fetch(jnp.stack([schur[:, half:], lcol1]), half)
    lower_b = paired[1]
    update = paired[0] - matmul(lower_b, lower_b.T)
    chol2 = jnp.linalg.cholesky(update)
    inv2 = jax.scipy.linalg.solve_triangular(chol2, identity, lower=True)
    remain = schur[:, half:] - matmul(lcol1, lower_b.T)
    lcol2 = matmul(remain, inv2.T)
    own_two = lax.dynamic_slice_in_dim(chol2, jnp.clip(first - half, 0, half - rows), rows, 0)
    lcol2 = jnp.where(first < width, own_two, lcol2)
    lcol2 = jnp.where(first < half, jnp.zeros_like(lcol2), lcol2)
    return jnp.concatenate([lcol1, lcol2], axis=1)


F32 = jnp.float32
BF16 = jnp.bfloat16
STEPS = 3
SETTLED = 1.6e-5


def split(x):
    high = x.astype(BF16)
    return high, (x - high.astype(F32)).astype(BF16)


def dot(a, b, contract=((1,), (0,))):
    return lax.dot_general(a, b, (contract, ((), ())), preferred_element_type=F32)


def dot3(a, b, contract=((1,), (0,))):
    (a_high, a_low), (b_high, b_low) = a, b
    return (
        dot(a_high, b_high, contract) + dot(a_high, b_low, contract) + dot(a_low, b_high, contract)
    )


NT = ((1,), (1,))


def kernel(
    n_scen,
    n_col,
    quarter,
    sub,
    lag,
    inv_hbm,
    coup_hbm,
    mask_ref,
    hess_ref,
    out_ref,
    flag_ref,
    inv,
    coup,
    high_t,
    low_t,
    prod,
    prod_high,
    prod_low,
    contrib,
    pair_slots,
    slots,
    plane_own,
    plane_pair,
    plane_slots,
    corner,
    scaled_high,
    scaled_low,
    y,
    y_next,
    y_high,
    y_low,
    solve_in,
    solve_out,
    back,
    late_out,
    load_sem,
    ring_send,
    ring_recv,
    pair_send,
    pair_recv,
    sum_send,
    sum_recv,
    plane_pair_send,
    plane_pair_recv,
    plane_send,
    plane_recv,
    fill_send,
    fill_recv,
    fill_pair_send,
    fill_pair_recv,
    in_send,
    in_recv,
    back_send,
    back_recv,
    late_send,
    late_recv,
):
    me = lax.axis_index("scen")
    z = lax.axis_index("col")
    depth = coup.shape[0]
    block = coup.shape[1]
    width = corner.shape[3]
    chunk = prod.shape[2]
    n_chunk = prod.shape[0]
    rows = block // n_scen
    piece = width // n_scen
    owners = width // rows
    tile = depth // mask_ref.shape[1]
    half = depth // 2
    n_sub = half // sub
    nb = width // 2
    n_chip = n_scen // 2
    chip = me // 2
    core = lax.rem(me, 2)
    other = 1 - core
    partner = chip * 2 + other

    barrier = pltpu.get_barrier_semaphore()

    coup_panel = pltpu.make_async_copy(
        coup_hbm.at[0, :, pl.ds(0, width)], coup.at[:, pl.ds(0, width)], load_sem.at[0]
    )
    coup_rest = pltpu.make_async_copy(
        coup_hbm.at[0, :, pl.ds(width, block - width)],
        coup.at[:, pl.ds(width, block - width)],
        load_sem.at[1],
    )
    inv_load = pltpu.make_async_copy(inv_hbm.at[0], inv, load_sem.at[2])
    coup_panel.start()

    @pl.when(z == 0)
    def _():
        inv_load.start()

    coup_rest.start()

    def greet_scen(k, _):
        pl.semaphore_signal(
            barrier,
            inc=1,
            device_id={"scen": lax.rem(me + k, n_scen)},
            device_id_type=pl.DeviceIdType.MESH,
        )
        return 0

    def greet_col(k, _):
        pl.semaphore_signal(
            barrier,
            inc=1,
            device_id={"col": lax.rem(z + k, n_col)},
            device_id_type=pl.DeviceIdType.MESH,
        )
        return 0

    lax.fori_loop(1, n_scen, greet_scen, 0)
    lax.fori_loop(1, n_col, greet_col, 0)
    pl.semaphore_wait(barrier, n_scen + n_col - 2)

    def ring_copy(way, g):
        s = lax.rem(g, n_sub)
        at = prod.at[g // n_sub, pl.ds(pl.multiple_of(way * half + s * sub, sub), sub), :]
        to = lax.rem(z + 1, n_col) if way == 0 else lax.rem(z + n_col - 1, n_col)
        return pltpu.make_async_remote_copy(
            src_ref=at,
            dst_ref=at,
            send_sem=ring_send.at[way, g],
            recv_sem=ring_recv.at[way, g],
            device_id={"col": to},
            device_id_type=pl.DeviceIdType.MESH,
        )

    def transpose_coupling(first, count):
        @pl.loop(0, depth // 128)
        def _(t):
            at = pl.ds(pl.multiple_of(t * 128, 128), 128)
            high, low = split(coup[at, pl.ds(first, count)].T)
            high_t[pl.ds(first, count), at] = high
            low_t[pl.ds(first, count), at] = low

    def split_prod(q):
        high, low = split(prod[q])
        prod_high[...] = high
        prod_low[...] = low

    per = quarter // rows // 2

    def pair_copy(q, r):
        at = pl.ds(pl.multiple_of(r * per, per), per)
        return pltpu.make_async_remote_copy(
            src_ref=contrib.at[q, at, other],
            dst_ref=pair_slots.at[q, at],
            send_sem=pair_send.at[q],
            recv_sem=pair_recv.at[q, r],
            device_id={"scen": partner},
            device_id_type=pl.DeviceIdType.MESH,
        )

    def form(q, r):
        at = pl.ds(pl.multiple_of(r * quarter, quarter), quarter)
        term = dot3((high_t[at, :], low_t[at, :]), (prod_high[...], prod_low[...]))
        contrib[q, pl.ds(pl.multiple_of(r * per, per), per)] = term.reshape(per, 2, rows, chunk)
        pair_copy(q, r).start()

    def pass_on(q, r):
        pair_copy(q, r).wait_recv()
        at = pl.ds(pl.multiple_of(r * per, per), per)
        contrib[q, at, core] = contrib[q, at, core] + pair_slots[q, at]

        def start(k, _):
            to = lax.rem(chip + k, per) + r * per

            @pl.when(to != chip)
            def _():
                pltpu.make_async_remote_copy(
                    src_ref=contrib.at[q, to, core],
                    dst_ref=slots.at[q, lax.rem(chip - to + n_chip, n_chip) - 1],
                    send_sem=sum_send.at[q],
                    recv_sem=sum_recv.at[q],
                    device_id={"scen": to * 2 + core},
                    device_id_type=pl.DeviceIdType.MESH,
                ).start()

            return 0

        lax.fori_loop(0, per, start, 0)

    def own_rows(q):
        own = contrib[q, chip, core]
        return lax.fori_loop(0, n_chip - 1, lambda k, total: total + slots[q, k], own)

    def in_copy(slot):
        return pltpu.make_async_remote_copy(
            src_ref=solve_in.at[slot],
            dst_ref=solve_in.at[slot],
            send_sem=in_send,
            recv_sem=in_recv,
            device_id={"col": 0},
            device_id_type=pl.DeviceIdType.MESH,
        )

    def back_copy(to):
        return pltpu.make_async_remote_copy(
            src_ref=solve_out.at[to],
            dst_ref=back,
            send_sem=back_send,
            recv_sem=back_recv,
            device_id={"col": to},
            device_id_type=pl.DeviceIdType.MESH,
        )

    @pl.when(z == 0)
    def _():
        coup_panel.wait()
        transpose_coupling(0, width)
        inv_load.wait()
        keep = jnp.concatenate(
            [
                jnp.full((tile, 1), mask_ref[0, t], jnp.int32).astype(F32)
                for t in range(mask_ref.shape[1])
            ],
            axis=0,
        )

        for q in range(n_chunk):
            panel = split(coup[:, pl.ds(q * chunk, chunk)] * keep)
            for r in range(depth // quarter):
                n_half = half // quarter
                r = (r % 2) * n_half + r // 2
                kept = inv[pl.ds(r * quarter, quarter), :]
                scale = keep[r * quarter : (r + 1) * quarter]
                prod[q, pl.ds(r * quarter, quarter), :] = dot3(split(kept), panel) * scale
                way = r // n_half
                for s in range(quarter // sub):
                    ring_copy(way, q * n_sub + (r % n_half) * (quarter // sub) + s).start()

        def plane_pair_copy(part):
            return pltpu.make_async_remote_copy(
                src_ref=plane_own.at[part, :, other],
                dst_ref=plane_pair.at[part],
                send_sem=plane_pair_send.at[part],
                recv_sem=plane_pair_recv.at[part],
                device_id={"scen": partner},
                device_id_type=pl.DeviceIdType.MESH,
            )

        def plane_form(part):
            group = quarter // piece // 2
            for q in range(n_chunk):
                split_prod(q)
                for r in range(width // quarter):
                    at = pl.ds(part * width + r * quarter, quarter)
                    term = dot3((high_t[at, :], low_t[at, :]), (prod_high[...], prod_low[...]))
                    plane_own[part, pl.ds(r * group, group), :, :, pl.ds(q * chunk, chunk)] = (
                        term.reshape(group, 2, piece, chunk)
                    )
            plane_pair_copy(part).start()

        def plane_pass_on(part):
            plane_pair_copy(part).wait_recv()
            step = max(1, n_chip // 4)
            for r in range(0, n_chip, step):
                at = pl.ds(r, step)
                plane_own[part, at, core] = plane_own[part, at, core] + plane_pair[part, at]

            def start(k, _):
                to = lax.rem(chip + k, n_chip)
                pltpu.make_async_remote_copy(
                    src_ref=plane_own.at[part, to, core],
                    dst_ref=plane_slots.at[part, n_chip - 1 - k],
                    send_sem=plane_send.at[part],
                    recv_sem=plane_recv.at[part],
                    device_id={"scen": to * 2 + core},
                    device_id_type=pl.DeviceIdType.MESH,
                ).start()
                return 0

            lax.fori_loop(1, n_chip, start, 0)

        def plane_total(part):
            some = plane_slots.at[part]
            pltpu.make_async_copy(some, some, plane_recv.at[part]).wait()
            return lax.fori_loop(
                0,
                n_chip - 1,
                lambda k, total: total + plane_slots[part, k],
                plane_own[part, chip, core],
            )

        plane_form(0)
        coup_rest.wait()
        transpose_coupling(width, block - width)
        plane_pass_on(0)
        plane_form(1)
        total = plane_total(0)
        row = me * piece + lax.broadcasted_iota(jnp.int32, (piece, width), 0)
        column = lax.broadcasted_iota(jnp.int32, (piece, width), 1)
        corner[chip, core] = total + jnp.where(row == column, hess_ref[...], 0.0)

        def fill_copy(k):
            return pltpu.make_async_remote_copy(
                src_ref=corner.at[chip, core],
                dst_ref=corner.at[chip, core],
                send_sem=fill_send,
                recv_sem=fill_recv.at[n_chip - 1 - k],
                device_id={"scen": lax.rem(chip + k, n_chip) * 2 + core},
                device_id_type=pl.DeviceIdType.MESH,
            )

        def hand_copy(k, which):
            at = corner.at[lax.rem(chip + k, n_chip), which]
            return pltpu.make_async_remote_copy(
                src_ref=at,
                dst_ref=at,
                send_sem=fill_pair_send,
                recv_sem=fill_pair_recv.at[k],
                device_id={"scen": partner},
                device_id_type=pl.DeviceIdType.MESH,
            )

        def fill_start(k, _):
            fill_copy(k).start()
            return 0

        hand_copy(0, core).start()
        lax.fori_loop(1, n_chip, fill_start, 0)

        def fill_hand(k, _):
            theirs = corner.at[lax.rem(chip + k, n_chip), core]
            pltpu.make_async_copy(theirs, theirs, fill_recv.at[k - 1]).wait()
            hand_copy(k, core).start()
            return 0

        lax.fori_loop(1, n_chip, fill_hand, 0)

        def hand_wait(k, _):
            hand_copy(k, other).wait_recv()
            return 0

        lax.fori_loop(0, n_chip, hand_wait, 0)
        plane_pass_on(1)

        row = lax.broadcasted_iota(jnp.int32, (width, width), 0)
        column = lax.broadcasted_iota(jnp.int32, (width, width), 1)
        whole = corner[...].reshape(width, width)
        on_diagonal = jnp.where(row == column, whole, 0.0)
        root_row = lax.rsqrt(jnp.sum(on_diagonal, axis=0, keepdims=True))
        root_column = lax.rsqrt(jnp.sum(on_diagonal, axis=1, keepdims=True))
        scaled = whole * root_column * root_row
        high, low = split(scaled)
        scaled_high[...] = high
        scaled_low[...] = low
        y[...] = jnp.where(row == column, 1.0, jnp.where(row > column, -scaled, 0.0))

        for step in range(STEPS):
            high, low = split(y[...])
            y_high[...] = high
            y_low[...] = low
            size = jnp.zeros((1, 1), F32)
            for r in range(2):
                at = pl.ds(r * nb, nb)
                to = pl.ds(0, (r + 1) * nb)
                t = dot3((y_high[at, to], y_low[at, to]), (scaled_high[to, to], scaled_low[to, to]))
                e = dot3(split(t), (y_high[to, to], y_low[to, to]), NT)
                e_row = r * nb + lax.broadcasted_iota(jnp.int32, e.shape, 0)
                e_column = lax.broadcasted_iota(jnp.int32, e.shape, 1)
                e = jnp.where(e_row == e_column, e - 1.0, jnp.where(e_row > e_column, e, 0.0))
                if step == STEPS - 1:
                    size = size + jnp.sum(e * e, keepdims=True)
                e = jnp.where(e_row == e_column, 0.5 * e, e)
                y_next[at, to] = y[at, to] - dot3(split(e), (y_high[to, to], y_low[to, to]))
            for r in range(2):
                at = pl.ds(r * nb, nb)
                to = pl.ds(0, (r + 1) * nb)
                y[at, to] = y_next[at, to]

        bad = jnp.where(size < SETTLED, 0.0, 1.0)
        y_final = split(y[...])

        later = plane_total(1) * root_row
        late_out[1, 0] = dot3(split(later), y_final, NT)
        late_to = owners + me * piece // rows
        late_part = lax.rem(me, rows // piece)

        def late_copy():
            return pltpu.make_async_remote_copy(
                src_ref=late_out.at[1, 0],
                dst_ref=late_out.at[0, late_part],
                send_sem=late_send,
                recv_sem=late_recv.at[late_part],
                device_id={"scen": late_to},
                device_id_type=pl.DeviceIdType.MESH,
            )

        @pl.when(late_to != me)
        def _():
            late_copy().start()

        rest = solve_in.at[pl.ds(1, n_col - 1)]
        pltpu.make_async_copy(rest, rest, in_recv).wait()
        given = solve_in[pl.ds(1, n_col - 1)].reshape((n_col - 1) * rows, width) * root_row
        solved = dot3(split(given), y_final, NT).reshape(n_col - 1, rows, width)
        solve_out[pl.ds(1, n_col - 1), pl.ds(0, rows), :] = solved
        solve_out[pl.ds(1, n_col - 1), pl.ds(rows, 8), :] = jnp.broadcast_to(
            bad, (n_col - 1, 8, width)
        )

        def back_start(k, _):
            back_copy(k).start()
            return 0

        lax.fori_loop(1, n_col, back_start, 0)

        @pl.when(me < owners)
        def _():
            chips = rows // piece // 2
            given = corner[pl.ds(lax.rem(me, owners) * chips, chips)].reshape(rows, width)
            row = me * rows + lax.broadcasted_iota(jnp.int32, (rows, width), 0)
            column = lax.broadcasted_iota(jnp.int32, (rows, width), 1)
            solved = dot3(split(given * root_row), y_final, NT)
            out_ref[...] = jnp.where(column <= row, solved, 0.0)

        @pl.when(me >= owners)
        def _():
            for part in range(rows // piece):

                @pl.when(jnp.logical_and(late_to == me, late_part == part))
                def _():
                    out_ref[pl.ds(part * piece, piece), :] = late_out[1, 0]

                @pl.when(jnp.logical_not(jnp.logical_and(late_to == me, late_part == part)))
                def _():
                    some = late_out.at[0, part]
                    pltpu.make_async_copy(some, some, late_recv.at[part]).wait()
                    out_ref[pl.ds(part * piece, piece), :] = late_out[0, part]

        flag_ref[...] = jnp.broadcast_to(bad, flag_ref.shape)

        @pl.loop(0, n_chunk * n_sub)
        def _(g):
            ring_copy(0, g).wait_send()
            ring_copy(1, g).wait_send()

        for part in range(2):
            plane_pair_copy(part).wait_send()
            some = plane_slots.at[part]
            pltpu.make_async_copy(some, some, plane_send.at[part]).wait()
        some = corner.at[pl.ds(1, n_chip - 1), 0]
        pltpu.make_async_copy(some, some, fill_send).wait()
        some = corner.at[:, 0]
        pltpu.make_async_copy(some, some, fill_pair_send).wait()

        @pl.when(late_to != me)
        def _():
            late_copy().wait_send()

        some = solve_out.at[pl.ds(1, n_col - 1)]
        pltpu.make_async_copy(some, some, back_send).wait()

    @pl.when(z != 0)
    def _():
        coup_panel.wait()
        coup_rest.wait()
        transpose_coupling(0, block)

        late = lag * jnp.maximum(z - 1, n_col - 1 - z)
        n_piece = n_chunk * n_sub
        n_row = block // quarter

        @pl.loop(0, n_piece + late)
        def _(t):
            g = t - lag * (z - 1)

            @pl.when(jnp.logical_and(g >= 0, g < n_piece))
            def _():
                up = ring_copy(0, g)
                up.wait_recv()

                @pl.when(z < n_col - 1)
                def _():
                    up.start()

            h = t - lag * (n_col - 1 - z)

            @pl.when(jnp.logical_and(h >= 0, h < n_piece))
            def _():
                down = ring_copy(1, h)
                down.wait_recv()

                @pl.when(z > 1)
                def _():
                    down.start()

            done = t - late + 1
            q = done // n_sub - 1
            r = lax.rem(done, n_sub)
            whole = done >= n_sub

            @pl.when(jnp.logical_and(whole, r == 0))
            def _():
                split_prod(q)

            inside = jnp.logical_and(whole, done < n_piece)

            @pl.when(jnp.logical_and(inside, r < n_row))
            def _():
                form(q, r)

            @pl.when(jnp.logical_and(inside, jnp.logical_and(r >= 1, r <= n_row)))
            def _():
                pass_on(q, r - 1)

        form(n_chunk - 1, 0)

        @pl.loop(1, n_row)
        def _(r):
            form(n_chunk - 1, r)
            pass_on(n_chunk - 1, r - 1)

        pass_on(n_chunk - 1, n_row - 1)

        for q in range(n_chunk):
            pltpu.make_async_copy(slots.at[q], slots.at[q], sum_recv.at[q]).wait()
            solve_in[z, :, pl.ds(q * chunk, chunk)] = own_rows(q)
        in_copy(z).start()

        for q in range(n_chunk):

            pltpu.make_async_copy(slots.at[q], slots.at[q], sum_send.at[q]).wait()
            pltpu.make_async_copy(pair_slots.at[q], pair_slots.at[q], pair_send.at[q]).wait()
        in_copy(z).wait_send()

        @pl.loop(0, n_piece)
        def _(g):
            @pl.when(z < n_col - 1)
            def _():
                ring_copy(0, g).wait_send()

            @pl.when(z > 1)
            def _():
                ring_copy(1, g).wait_send()

        pltpu.make_async_copy(back, back, back_recv).wait()
        out_ref[...] = back[pl.ds(0, rows), :]
        flag_ref[...] = back[pl.ds(rows, 8), pl.ds(0, 128)]


def fused(inverses, coupling, tile_mask, hess_diag, quarter=256, chunk=256, sub=64, lag=3):
    n_scen = lax.axis_size("scen")
    n_col = lax.axis_size("col")
    _, depth, block = coupling.shape
    width = hess_diag.shape[0]
    rows = block // n_scen
    piece = width // n_scen
    n_chunk = width // chunk
    n_sub = depth // 2 // sub
    vmem = pltpu.VMEM
    dma = pltpu.SemaphoreType.DMA
    scratch = [
        vmem((depth, depth), F32),
        vmem((depth, block), F32),
        vmem((block, depth), BF16),
        vmem((block, depth), BF16),
        vmem((n_chunk, depth, chunk), F32),
        vmem((depth, chunk), BF16),
        vmem((depth, chunk), BF16),
        vmem((n_chunk, n_scen // 2, 2, rows, chunk), F32),
        vmem((n_chunk, n_scen // 2, rows, chunk), F32),
        vmem((n_chunk, n_scen // 2 - 1, rows, chunk), F32),
        vmem((2, n_scen // 2, 2, piece, width), F32),
        vmem((2, n_scen // 2, piece, width), F32),
        vmem((2, n_scen // 2 - 1, piece, width), F32),
        vmem((n_scen // 2, 2, piece, width), F32),
        vmem((width, width), BF16),
        vmem((width, width), BF16),
        vmem((width, width), F32),
        vmem((width, width), F32),
        vmem((width, width), BF16),
        vmem((width, width), BF16),
        vmem((n_col, rows, width), F32),
        vmem((n_col, rows + 8, width), F32),
        vmem((rows + 8, width), F32),
        vmem((2, rows // piece, piece, width), F32),
        dma((3,)),
        dma((2, n_chunk * n_sub)),
        dma((2, n_chunk * n_sub)),
        dma((n_chunk,)),
        dma((n_chunk, block // quarter)),
        dma((n_chunk,)),
        dma((n_chunk,)),
        dma((2,)),
        dma((2,)),
        dma((2,)),
        dma((2,)),
        dma(()),
        dma((n_scen // 2 - 1,)),
        dma(()),
        dma((n_scen // 2,)),
        dma(()),
        dma(()),
        dma(()),
        dma(()),
        dma(()),
        dma((rows // piece,)),
    ]
    return pl.pallas_call(
        functools.partial(kernel, n_scen, n_col, quarter, sub, lag),
        out_shape=(
            jax.ShapeDtypeStruct((rows, width), F32),
            jax.ShapeDtypeStruct((8, 128), F32),
        ),
        in_specs=[
            pl.BlockSpec(memory_space=pl.ANY),
            pl.BlockSpec(memory_space=pl.ANY),
            pl.BlockSpec(memory_space=pltpu.SMEM),
            pl.BlockSpec(memory_space=pltpu.VMEM),
        ],
        out_specs=[pl.BlockSpec(memory_space=pltpu.VMEM)] * 2,
        scratch_shapes=scratch,
        compiler_params=pltpu.CompilerParams(
            collective_id=0, has_side_effects=True, vmem_limit_bytes=50 * 2**20
        ),
    )(inverses, coupling, tile_mask, hess_diag[None, :])


def body(inverses, coupling, tile_mask, hess_diag):
    factor, flag = fused(inverses, coupling, tile_mask, hess_diag)
    return lax.cond(
        flag[0, 0] > 0.5,
        direct_body,
        lambda *_: factor,
        inverses,
        coupling,
        tile_mask,
        hess_diag,
    )


def solution(mesh):
    in_specs = (P("scen", None, None), P("scen", None, "col"), P("scen", None), P())
    out_specs = P(("col", "scen"), None)
    return jax.shard_map(body, mesh=mesh, in_specs=in_specs, out_specs=out_specs, check_vma=False)
```

```python
import functools

import jax
import jax.numpy as jnp
from jax import lax
from jax.experimental import pallas as pl
from jax.experimental.pallas import tpu as pltpu
from jax.sharding import PartitionSpec as P


def from_first(x, axis):
    at = lax.axis_index(axis)
    have = 1
    while have < lax.axis_size(axis):
        pairs = [(i, i + have) for i in range(min(have, lax.axis_size(axis) - have))]
        got = lax.ppermute(x, axis, pairs)
        x = jnp.where(jnp.logical_and(at >= have, at < 2 * have), got, x)
        have *= 2
    return x


def in_blocks(x, dim, size):
    lengths = x.shape
    blocks = x.reshape(*lengths[:dim], size, lengths[dim] // size, *lengths[dim + 1 :])
    return jnp.moveaxis(blocks, dim, 0)


def sum_at_owner(x, axis, dim):
    size = lax.axis_size(axis)
    blocks = lax.all_to_all(in_blocks(x, dim, size), axis, 0, 0, tiled=True)
    return jnp.sum(blocks, axis=0)


def sent_to_all(x, axis):
    size = lax.axis_size(axis)
    return lax.all_to_all(jnp.broadcast_to(x[None], (size, *x.shape)), axis, 0, 0, tiled=True)


def in_order(blocks, dim):
    lengths = list(blocks.shape[1:])
    lengths[dim] *= blocks.shape[0]
    return jnp.moveaxis(blocks, 0, dim).reshape(lengths)


def collect(x, axis, dim):
    blocks = sent_to_all(x, axis)
    return in_order(blocks, dim)


def outer_rows(left, piece):
    return lax.dot_general(
        left,
        piece,
        (((0,), (0,)), ((), ())),
        precision=lax.Precision.HIGHEST,
        preferred_element_type=jnp.float32,
    )


def matmul(left, right):
    return jnp.dot(left, right, precision=lax.Precision.HIGHEST, preferred_element_type=jnp.float32)


def direct_body(inverses, coupling, tile_mask, hess_diag):
    inverse = inverses[0]
    local = coupling[0]
    width = hess_diag.shape[0]
    half = width // 2
    scen_size = lax.axis_size("scen")
    rows = local.shape[1] // scen_size
    row_keep = jnp.repeat(tile_mask[0].astype(jnp.float32), local.shape[0] // tile_mask.shape[1])
    panel = from_first(local[:, :width], "col")
    panel = panel * row_keep[:, None]
    product = matmul(inverse, panel) * row_keep[:, None]
    block = local
    summed = sum_at_owner(outer_rows(block, product), "scen", 0)
    first = lax.axis_index("col") * local.shape[1] + lax.axis_index("scen") * rows
    global_rows = first + jnp.arange(rows, dtype=jnp.int32)
    columns = jnp.arange(width, dtype=jnp.int32)
    schur = summed + jnp.where(columns[None, :] == global_rows[:, None], hess_diag[None, :], 0.0)

    def fetch(stacked, low):
        whole = collect(stacked, "scen", 1)
        block = whole[:, low : low + half]
        return from_first(block, "col")

    identity = jnp.eye(half, dtype=jnp.float32)
    block_one = fetch(schur[None, :, :half], 0)[0]
    chol1 = jnp.linalg.cholesky(block_one)
    inv1 = jax.scipy.linalg.solve_triangular(chol1, identity, lower=True)
    lcol1 = matmul(schur[:, :half], inv1.T)
    own_one = lax.dynamic_slice_in_dim(chol1, jnp.clip(first, 0, half - rows), rows, 0)
    lcol1 = jnp.where(first < half, own_one, lcol1)
    paired = fetch(jnp.stack([schur[:, half:], lcol1]), half)
    lower_b = paired[1]
    update = paired[0] - matmul(lower_b, lower_b.T)
    chol2 = jnp.linalg.cholesky(update)
    inv2 = jax.scipy.linalg.solve_triangular(chol2, identity, lower=True)
    remain = schur[:, half:] - matmul(lcol1, lower_b.T)
    lcol2 = matmul(remain, inv2.T)
    own_two = lax.dynamic_slice_in_dim(chol2, jnp.clip(first - half, 0, half - rows), rows, 0)
    lcol2 = jnp.where(first < width, own_two, lcol2)
    lcol2 = jnp.where(first < half, jnp.zeros_like(lcol2), lcol2)
    return jnp.concatenate([lcol1, lcol2], axis=1)


F32 = jnp.float32
BF16 = jnp.bfloat16
STEPS = 3
SETTLED = 1.6e-5


def split(x):
    high = x.astype(BF16)
    return high, (x - high.astype(F32)).astype(BF16)


def dot(a, b, contract=((1,), (0,))):
    return lax.dot_general(a, b, (contract, ((), ())), preferred_element_type=F32)


def dot3(a, b, contract=((1,), (0,))):
    (a_high, a_low), (b_high, b_low) = a, b
    return (
        dot(a_high, b_high, contract) + dot(a_high, b_low, contract) + dot(a_low, b_high, contract)
    )


NT = ((1,), (1,))


def kernel(
    n_scen,
    n_col,
    quarter,
    sub,
    lag,
    inv_hbm,
    coup_hbm,
    mask_ref,
    hess_ref,
    out_ref,
    flag_ref,
    inv,
    coup,
    high_t,
    low_t,
    prod,
    prod_high,
    prod_low,
    contrib,
    pair_slots,
    slots,
    plane_own,
    plane_pair,
    plane_slots,
    corner,
    scaled_high,
    scaled_low,
    y,
    y_next,
    y_high,
    y_low,
    solve_in,
    solve_out,
    back,
    late_out,
    load_sem,
    ring_send,
    ring_recv,
    pair_send,
    pair_recv,
    sum_send,
    sum_recv,
    plane_pair_send,
    plane_pair_recv,
    plane_send,
    plane_recv,
    fill_send,
    fill_recv,
    fill_pair_send,
    fill_pair_recv,
    in_send,
    in_recv,
    back_send,
    back_recv,
    late_send,
    late_recv,
):
    me = lax.axis_index("scen")
    z = lax.axis_index("col")
    depth = coup.shape[0]
    block = coup.shape[1]
    width = corner.shape[3]
    chunk = prod.shape[2]
    n_chunk = prod.shape[0]
    rows = block // n_scen
    piece = width // n_scen
    owners = width // rows
    tile = depth // mask_ref.shape[1]
    half = depth // 2
    n_sub = half // sub
    nb = width // 2
    n_chip = n_scen // 2
    chip = me // 2
    core = lax.rem(me, 2)
    other = 1 - core
    partner = chip * 2 + other

    barrier = pltpu.get_barrier_semaphore()

    coup_panel = pltpu.make_async_copy(
        coup_hbm.at[0, :, pl.ds(0, width)], coup.at[:, pl.ds(0, width)], load_sem.at[0]
    )
    coup_rest = pltpu.make_async_copy(
        coup_hbm.at[0, :, pl.ds(width, block - width)],
        coup.at[:, pl.ds(width, block - width)],
        load_sem.at[1],
    )
    inv_load = pltpu.make_async_copy(inv_hbm.at[0], inv, load_sem.at[2])
    coup_panel.start()

    @pl.when(z == 0)
    def _():
        inv_load.start()

    coup_rest.start()

    def greet_scen(k, _):
        pl.semaphore_signal(
            barrier,
            inc=1,
            device_id={"scen": lax.rem(me + k, n_scen)},
            device_id_type=pl.DeviceIdType.MESH,
        )
        return 0

    def greet_col(k, _):
        pl.semaphore_signal(
            barrier,
            inc=1,
            device_id={"col": lax.rem(z + k, n_col)},
            device_id_type=pl.DeviceIdType.MESH,
        )
        return 0

    lax.fori_loop(1, n_scen, greet_scen, 0)
    lax.fori_loop(1, n_col, greet_col, 0)
    pl.semaphore_wait(barrier, n_scen + n_col - 2)

    def ring_copy(way, g):
        s = lax.rem(g, n_sub)
        at = prod.at[g // n_sub, pl.ds(pl.multiple_of(way * half + s * sub, sub), sub), :]
        to = lax.rem(z + 1, n_col) if way == 0 else lax.rem(z + n_col - 1, n_col)
        return pltpu.make_async_remote_copy(
            src_ref=at,
            dst_ref=at,
            send_sem=ring_send.at[way, g],
            recv_sem=ring_recv.at[way, g],
            device_id={"col": to},
            device_id_type=pl.DeviceIdType.MESH,
        )

    def transpose_coupling(first, count):
        @pl.loop(0, depth // 128)
        def _(t):
            at = pl.ds(pl.multiple_of(t * 128, 128), 128)
            high, low = split(coup[at, pl.ds(first, count)].T)
            high_t[pl.ds(first, count), at] = high
            low_t[pl.ds(first, count), at] = low

    def split_prod(q):
        high, low = split(prod[q])
        prod_high[...] = high
        prod_low[...] = low

    per = quarter // rows // 2

    def pair_copy(q, r):
        at = pl.ds(pl.multiple_of(r * per, per), per)
        return pltpu.make_async_remote_copy(
            src_ref=contrib.at[q, at, other],
            dst_ref=pair_slots.at[q, at],
            send_sem=pair_send.at[q],
            recv_sem=pair_recv.at[q, r],
            device_id={"scen": partner},
            device_id_type=pl.DeviceIdType.MESH,
        )

    def form(q, r):
        at = pl.ds(pl.multiple_of(r * quarter, quarter), quarter)
        term = dot3((high_t[at, :], low_t[at, :]), (prod_high[...], prod_low[...]))
        contrib[q, pl.ds(pl.multiple_of(r * per, per), per)] = term.reshape(per, 2, rows, chunk)
        pair_copy(q, r).start()

    def pass_on(q, r):
        pair_copy(q, r).wait_recv()
        at = pl.ds(pl.multiple_of(r * per, per), per)
        contrib[q, at, core] = contrib[q, at, core] + pair_slots[q, at]

        def start(k, _):
            to = lax.rem(chip + k, per) + r * per

            @pl.when(to != chip)
            def _():
                pltpu.make_async_remote_copy(
                    src_ref=contrib.at[q, to, core],
                    dst_ref=slots.at[q, lax.rem(chip - to + n_chip, n_chip) - 1],
                    send_sem=sum_send.at[q],
                    recv_sem=sum_recv.at[q],
                    device_id={"scen": to * 2 + core},
                    device_id_type=pl.DeviceIdType.MESH,
                ).start()

            return 0

        lax.fori_loop(0, per, start, 0)

    def own_rows(q):
        own = contrib[q, chip, core]
        return lax.fori_loop(0, n_chip - 1, lambda k, total: total + slots[q, k], own)

    def in_copy(slot):
        return pltpu.make_async_remote_copy(
            src_ref=solve_in.at[slot],
            dst_ref=solve_in.at[slot],
            send_sem=in_send,
            recv_sem=in_recv,
            device_id={"col": 0},
            device_id_type=pl.DeviceIdType.MESH,
        )

    def back_copy(to):
        return pltpu.make_async_remote_copy(
            src_ref=solve_out.at[to],
            dst_ref=back,
            send_sem=back_send,
            recv_sem=back_recv,
            device_id={"col": to},
            device_id_type=pl.DeviceIdType.MESH,
        )

    @pl.when(z == 0)
    def _():
        coup_panel.wait()
        transpose_coupling(0, width)
        inv_load.wait()
        keep = jnp.concatenate(
            [
                jnp.full((tile, 1), mask_ref[0, t], jnp.int32).astype(F32)
                for t in range(mask_ref.shape[1])
            ],
            axis=0,
        )

        for q in range(n_chunk):
            panel = split(coup[:, pl.ds(q * chunk, chunk)] * keep)
            for r in range(depth // quarter):
                n_half = half // quarter
                r = (r % 2) * n_half + r // 2
                kept = inv[pl.ds(r * quarter, quarter), :]
                scale = keep[r * quarter : (r + 1) * quarter]
                prod[q, pl.ds(r * quarter, quarter), :] = dot3(split(kept), panel) * scale
                way = r // n_half
                for s in range(quarter // sub):
                    ring_copy(way, q * n_sub + (r % n_half) * (quarter // sub) + s).start()

        def plane_pair_copy(part):
            return pltpu.make_async_remote_copy(
                src_ref=plane_own.at[part, :, other],
                dst_ref=plane_pair.at[part],
                send_sem=plane_pair_send.at[part],
                recv_sem=plane_pair_recv.at[part],
                device_id={"scen": partner},
                device_id_type=pl.DeviceIdType.MESH,
            )

        def plane_form(part):
            group = quarter // piece // 2
            for q in range(n_chunk):
                split_prod(q)
                for r in range(width // quarter):
                    at = pl.ds(part * width + r * quarter, quarter)
                    term = dot3((high_t[at, :], low_t[at, :]), (prod_high[...], prod_low[...]))
                    plane_own[part, pl.ds(r * group, group), :, :, pl.ds(q * chunk, chunk)] = (
                        term.reshape(group, 2, piece, chunk)
                    )
            plane_pair_copy(part).start()

        def plane_pass_on(part):
            plane_pair_copy(part).wait_recv()
            step = max(1, n_chip // 4)
            for r in range(0, n_chip, step):
                at = pl.ds(r, step)
                plane_own[part, at, core] = plane_own[part, at, core] + plane_pair[part, at]

            def start(k, _):
                to = lax.rem(chip + k, n_chip)
                pltpu.make_async_remote_copy(
                    src_ref=plane_own.at[part, to, core],
                    dst_ref=plane_slots.at[part, n_chip - 1 - k],
                    send_sem=plane_send.at[part],
                    recv_sem=plane_recv.at[part],
                    device_id={"scen": to * 2 + core},
                    device_id_type=pl.DeviceIdType.MESH,
                ).start()
                return 0

            lax.fori_loop(1, n_chip, start, 0)

        def plane_total(part):
            some = plane_slots.at[part]
            pltpu.make_async_copy(some, some, plane_recv.at[part]).wait()
            return lax.fori_loop(
                0,
                n_chip - 1,
                lambda k, total: total + plane_slots[part, k],
                plane_own[part, chip, core],
            )

        plane_form(0)
        coup_rest.wait()
        transpose_coupling(width, block - width)
        plane_pass_on(0)
        plane_form(1)
        total = plane_total(0)
        row = me * piece + lax.broadcasted_iota(jnp.int32, (piece, width), 0)
        column = lax.broadcasted_iota(jnp.int32, (piece, width), 1)
        corner[chip, core] = total + jnp.where(row == column, hess_ref[...], 0.0)

        def fill_copy(k):
            return pltpu.make_async_remote_copy(
                src_ref=corner.at[chip, core],
                dst_ref=corner.at[chip, core],
                send_sem=fill_send,
                recv_sem=fill_recv.at[n_chip - 1 - k],
                device_id={"scen": lax.rem(chip + k, n_chip) * 2 + core},
                device_id_type=pl.DeviceIdType.MESH,
            )

        def hand_copy(k, which):
            at = corner.at[lax.rem(chip + k, n_chip), which]
            return pltpu.make_async_remote_copy(
                src_ref=at,
                dst_ref=at,
                send_sem=fill_pair_send,
                recv_sem=fill_pair_recv.at[k],
                device_id={"scen": partner},
                device_id_type=pl.DeviceIdType.MESH,
            )

        def fill_start(k, _):
            fill_copy(k).start()
            return 0

        hand_copy(0, core).start()
        lax.fori_loop(1, n_chip, fill_start, 0)

        def fill_hand(k, _):
            theirs = corner.at[lax.rem(chip + k, n_chip), core]
            pltpu.make_async_copy(theirs, theirs, fill_recv.at[k - 1]).wait()
            hand_copy(k, core).start()
            return 0

        lax.fori_loop(1, n_chip, fill_hand, 0)

        def hand_wait(k, _):
            hand_copy(k, other).wait_recv()
            return 0

        lax.fori_loop(0, n_chip, hand_wait, 0)
        plane_pass_on(1)

        row = lax.broadcasted_iota(jnp.int32, (width, width), 0)
        column = lax.broadcasted_iota(jnp.int32, (width, width), 1)
        whole = corner[...].reshape(width, width)
        on_diagonal = jnp.where(row == column, whole, 0.0)
        root_row = lax.rsqrt(jnp.sum(on_diagonal, axis=0, keepdims=True))
        root_column = lax.rsqrt(jnp.sum(on_diagonal, axis=1, keepdims=True))
        scaled = whole * root_column * root_row
        high, low = split(scaled)
        scaled_high[...] = high
        scaled_low[...] = low
        y[...] = jnp.where(row == column, 1.0, jnp.where(row > column, -scaled, 0.0))

        for step in range(STEPS):
            high, low = split(y[...])
            y_high[...] = high
            y_low[...] = low
            size = jnp.zeros((1, 1), F32)
            for r in range(2):
                at = pl.ds(r * nb, nb)
                to = pl.ds(0, (r + 1) * nb)
                t = dot3((y_high[at, to], y_low[at, to]), (scaled_high[to, to], scaled_low[to, to]))
                e = dot3(split(t), (y_high[to, to], y_low[to, to]), NT)
                e_row = r * nb + lax.broadcasted_iota(jnp.int32, e.shape, 0)
                e_column = lax.broadcasted_iota(jnp.int32, e.shape, 1)
                e = jnp.where(e_row == e_column, e - 1.0, jnp.where(e_row > e_column, e, 0.0))
                if step == STEPS - 1:
                    size = size + jnp.sum(e * e, keepdims=True)
                e = jnp.where(e_row == e_column, 0.5 * e, e)
                y_next[at, to] = y[at, to] - dot3(split(e), (y_high[to, to], y_low[to, to]))
            for r in range(2):
                at = pl.ds(r * nb, nb)
                to = pl.ds(0, (r + 1) * nb)
                y[at, to] = y_next[at, to]

        bad = jnp.where(size < SETTLED, 0.0, 1.0)
        y_final = split(y[...])

        later = plane_total(1) * root_row
        late_out[1, 0] = dot3(split(later), y_final, NT)
        late_to = owners + me * piece // rows
        late_part = lax.rem(me, rows // piece)

        def late_copy():
            return pltpu.make_async_remote_copy(
                src_ref=late_out.at[1, 0],
                dst_ref=late_out.at[0, late_part],
                send_sem=late_send,
                recv_sem=late_recv.at[late_part],
                device_id={"scen": late_to},
                device_id_type=pl.DeviceIdType.MESH,
            )

        @pl.when(late_to != me)
        def _():
            late_copy().start()

        rest = solve_in.at[pl.ds(1, n_col - 1)]
        pltpu.make_async_copy(rest, rest, in_recv).wait()
        given = solve_in[pl.ds(1, n_col - 1)].reshape((n_col - 1) * rows, width) * root_row
        solved = dot3(split(given), y_final, NT).reshape(n_col - 1, rows, width)
        solve_out[pl.ds(1, n_col - 1), pl.ds(0, rows), :] = solved
        solve_out[pl.ds(1, n_col - 1), pl.ds(rows, 8), :] = jnp.broadcast_to(
            bad, (n_col - 1, 8, width)
        )

        def back_start(k, _):
            back_copy(k).start()
            return 0

        lax.fori_loop(1, n_col, back_start, 0)

        @pl.when(me < owners)
        def _():
            chips = rows // piece // 2
            given = corner[pl.ds(lax.rem(me, owners) * chips, chips)].reshape(rows, width)
            row = me * rows + lax.broadcasted_iota(jnp.int32, (rows, width), 0)
            column = lax.broadcasted_iota(jnp.int32, (rows, width), 1)
            solved = dot3(split(given * root_row), y_final, NT)
            out_ref[...] = jnp.where(column <= row, solved, 0.0)

        @pl.when(me >= owners)
        def _():
            for part in range(rows // piece):

                @pl.when(jnp.logical_and(late_to == me, late_part == part))
                def _():
                    out_ref[pl.ds(part * piece, piece), :] = late_out[1, 0]

                @pl.when(jnp.logical_not(jnp.logical_and(late_to == me, late_part == part)))
                def _():
                    some = late_out.at[0, part]
                    pltpu.make_async_copy(some, some, late_recv.at[part]).wait()
                    out_ref[pl.ds(part * piece, piece), :] = late_out[0, part]

        flag_ref[...] = jnp.broadcast_to(bad, flag_ref.shape)

        @pl.loop(0, n_chunk * n_sub)
        def _(g):
            ring_copy(0, g).wait_send()
            ring_copy(1, g).wait_send()

        for part in range(2):
            plane_pair_copy(part).wait_send()
            some = plane_slots.at[part]
            pltpu.make_async_copy(some, some, plane_send.at[part]).wait()
        some = corner.at[pl.ds(1, n_chip - 1), 0]
        pltpu.make_async_copy(some, some, fill_send).wait()
        some = corner.at[:, 0]
        pltpu.make_async_copy(some, some, fill_pair_send).wait()

        @pl.when(late_to != me)
        def _():
            late_copy().wait_send()

        some = solve_out.at[pl.ds(1, n_col - 1)]
        pltpu.make_async_copy(some, some, back_send).wait()

    @pl.when(z != 0)
    def _():
        coup_panel.wait()
        coup_rest.wait()
        transpose_coupling(0, block)

        late = lag * jnp.maximum(z - 1, n_col - 1 - z)
        n_piece = n_chunk * n_sub
        n_row = block // quarter

        @pl.loop(0, n_piece + late)
        def _(t):
            g = t - lag * (z - 1)

            @pl.when(jnp.logical_and(g >= 0, g < n_piece))
            def _():
                up = ring_copy(0, g)
                up.wait_recv()

                @pl.when(z < n_col - 1)
                def _():
                    up.start()

            h = t - lag * (n_col - 1 - z)

            @pl.when(jnp.logical_and(h >= 0, h < n_piece))
            def _():
                down = ring_copy(1, h)
                down.wait_recv()

                @pl.when(z > 1)
                def _():
                    down.start()

            done = t - late + 1
            q = done // n_sub - 1
            r = lax.rem(done, n_sub)
            whole = done >= n_sub

            @pl.when(jnp.logical_and(whole, r == 0))
            def _():
                split_prod(q)

            inside = jnp.logical_and(whole, done < n_piece)

            @pl.when(jnp.logical_and(inside, r < n_row))
            def _():
                form(q, r)

            @pl.when(jnp.logical_and(inside, jnp.logical_and(r >= 1, r <= n_row)))
            def _():
                pass_on(q, r - 1)

        form(n_chunk - 1, 0)

        @pl.loop(1, n_row)
        def _(r):
            form(n_chunk - 1, r)
            pass_on(n_chunk - 1, r - 1)

        pass_on(n_chunk - 1, n_row - 1)

        for q in range(n_chunk):
            pltpu.make_async_copy(slots.at[q], slots.at[q], sum_recv.at[q]).wait()
            solve_in[z, :, pl.ds(q * chunk, chunk)] = own_rows(q)
        in_copy(z).start()

        for q in range(n_chunk):

            pltpu.make_async_copy(slots.at[q], slots.at[q], sum_send.at[q]).wait()
            pltpu.make_async_copy(pair_slots.at[q], pair_slots.at[q], pair_send.at[q]).wait()
        in_copy(z).wait_send()

        @pl.loop(0, n_piece)
        def _(g):
            @pl.when(z < n_col - 1)
            def _():
                ring_copy(0, g).wait_send()

            @pl.when(z > 1)
            def _():
                ring_copy(1, g).wait_send()

        pltpu.make_async_copy(back, back, back_recv).wait()
        out_ref[...] = back[pl.ds(0, rows), :]
        flag_ref[...] = back[pl.ds(rows, 8), pl.ds(0, 128)]


def fused(inverses, coupling, tile_mask, hess_diag, quarter=256, chunk=256, sub=64, lag=3):
    n_scen = lax.axis_size("scen")
    n_col = lax.axis_size("col")
    _, depth, block = coupling.shape
    width = hess_diag.shape[0]
    rows = block // n_scen
    piece = width // n_scen
    n_chunk = width // chunk
    n_sub = depth // 2 // sub
    vmem = pltpu.VMEM
    dma = pltpu.SemaphoreType.DMA
    scratch = [
        vmem((depth, depth), F32),
        vmem((depth, block), F32),
        vmem((block, depth), BF16),
        vmem((block, depth), BF16),
        vmem((n_chunk, depth, chunk), F32),
        vmem((depth, chunk), BF16),
        vmem((depth, chunk), BF16),
        vmem((n_chunk, n_scen // 2, 2, rows, chunk), F32),
        vmem((n_chunk, n_scen // 2, rows, chunk), F32),
        vmem((n_chunk, n_scen // 2 - 1, rows, chunk), F32),
        vmem((2, n_scen // 2, 2, piece, width), F32),
        vmem((2, n_scen // 2, piece, width), F32),
        vmem((2, n_scen // 2 - 1, piece, width), F32),
        vmem((n_scen // 2, 2, piece, width), F32),
        vmem((width, width), BF16),
        vmem((width, width), BF16),
        vmem((width, width), F32),
        vmem((width, width), F32),
        vmem((width, width), BF16),
        vmem((width, width), BF16),
        vmem((n_col, rows, width), F32),
        vmem((n_col, rows + 8, width), F32),
        vmem((rows + 8, width), F32),
        vmem((2, rows // piece, piece, width), F32),
        dma((3,)),
        dma((2, n_chunk * n_sub)),
        dma((2, n_chunk * n_sub)),
        dma((n_chunk,)),
        dma((n_chunk, block // quarter)),
        dma((n_chunk,)),
        dma((n_chunk,)),
        dma((2,)),
        dma((2,)),
        dma((2,)),
        dma((2,)),
        dma(()),
        dma((n_scen // 2 - 1,)),
        dma(()),
        dma((n_scen // 2,)),
        dma(()),
        dma(()),
        dma(()),
        dma(()),
        dma(()),
        dma((rows // piece,)),
    ]
    return pl.pallas_call(
        functools.partial(kernel, n_scen, n_col, quarter, sub, lag),
        out_shape=(
            jax.ShapeDtypeStruct((rows, width), F32),
            jax.ShapeDtypeStruct((8, 128), F32),
        ),
        in_specs=[
            pl.BlockSpec(memory_space=pl.ANY),
            pl.BlockSpec(memory_space=pl.ANY),
            pl.BlockSpec(memory_space=pltpu.SMEM),
            pl.BlockSpec(memory_space=pltpu.VMEM),
        ],
        out_specs=[pl.BlockSpec(memory_space=pltpu.VMEM)] * 2,
        scratch_shapes=scratch,
        compiler_params=pltpu.CompilerParams(
            collective_id=0, has_side_effects=True, vmem_limit_bytes=50 * 2**20
        ),
    )(inverses, coupling, tile_mask, hess_diag[None, :])


def body(inverses, coupling, tile_mask, hess_diag):
    factor, flag = fused(inverses, coupling, tile_mask, hess_diag)
    return lax.cond(
        flag[0, 0] > 0.5,
        direct_body,
        lambda *_: factor,
        inverses,
        coupling,
        tile_mask,
        hess_diag,
    )


def solution(mesh):
    in_specs = (P("scen", None, None), P("scen", None, "col"), P("scen", None), P())
    out_specs = P(("col", "scen"), None)
    return jax.shard_map(body, mesh=mesh, in_specs=in_specs, out_specs=out_specs, check_vma=False)
```

```python
import functools

import jax
import jax.numpy as jnp
from jax import lax
from jax.experimental import pallas as pl
from jax.experimental.pallas import tpu as pltpu
from jax.sharding import PartitionSpec as P


def from_first(x, axis):
    at = lax.axis_index(axis)
    have = 1
    while have < lax.axis_size(axis):
        pairs = [(i, i + have) for i in range(min(have, lax.axis_size(axis) - have))]
        got = lax.ppermute(x, axis, pairs)
        x = jnp.where(jnp.logical_and(at >= have, at < 2 * have), got, x)
        have *= 2
    return x


def in_blocks(x, dim, size):
    lengths = x.shape
    blocks = x.reshape(*lengths[:dim], size, lengths[dim] // size, *lengths[dim + 1 :])
    return jnp.moveaxis(blocks, dim, 0)


def sum_at_owner(x, axis, dim):
    size = lax.axis_size(axis)
    blocks = lax.all_to_all(in_blocks(x, dim, size), axis, 0, 0, tiled=True)
    return jnp.sum(blocks, axis=0)


def sent_to_all(x, axis):
    size = lax.axis_size(axis)
    return lax.all_to_all(jnp.broadcast_to(x[None], (size, *x.shape)), axis, 0, 0, tiled=True)


def in_order(blocks, dim):
    lengths = list(blocks.shape[1:])
    lengths[dim] *= blocks.shape[0]
    return jnp.moveaxis(blocks, 0, dim).reshape(lengths)


def collect(x, axis, dim):
    blocks = sent_to_all(x, axis)
    return in_order(blocks, dim)


def outer_rows(left, piece):
    return lax.dot_general(
        left,
        piece,
        (((0,), (0,)), ((), ())),
        precision=lax.Precision.HIGHEST,
        preferred_element_type=jnp.float32,
    )


def matmul(left, right):
    return jnp.dot(left, right, precision=lax.Precision.HIGHEST, preferred_element_type=jnp.float32)


def direct_body(inverses, coupling, tile_mask, hess_diag):
    inverse = inverses[0]
    local = coupling[0]
    width = hess_diag.shape[0]
    half = width // 2
    scen_size = lax.axis_size("scen")
    rows = local.shape[1] // scen_size
    row_keep = jnp.repeat(tile_mask[0].astype(jnp.float32), local.shape[0] // tile_mask.shape[1])
    panel = from_first(local[:, :width], "col")
    panel = panel * row_keep[:, None]
    product = matmul(inverse, panel) * row_keep[:, None]
    block = local
    summed = sum_at_owner(outer_rows(block, product), "scen", 0)
    first = lax.axis_index("col") * local.shape[1] + lax.axis_index("scen") * rows
    global_rows = first + jnp.arange(rows, dtype=jnp.int32)
    columns = jnp.arange(width, dtype=jnp.int32)
    schur = summed + jnp.where(columns[None, :] == global_rows[:, None], hess_diag[None, :], 0.0)

    def fetch(stacked, low):
        whole = collect(stacked, "scen", 1)
        block = whole[:, low : low + half]
        return from_first(block, "col")

    identity = jnp.eye(half, dtype=jnp.float32)
    block_one = fetch(schur[None, :, :half], 0)[0]
    chol1 = jnp.linalg.cholesky(block_one)
    inv1 = jax.scipy.linalg.solve_triangular(chol1, identity, lower=True)
    lcol1 = matmul(schur[:, :half], inv1.T)
    own_one = lax.dynamic_slice_in_dim(chol1, jnp.clip(first, 0, half - rows), rows, 0)
    lcol1 = jnp.where(first < half, own_one, lcol1)
    paired = fetch(jnp.stack([schur[:, half:], lcol1]), half)
    lower_b = paired[1]
    update = paired[0] - matmul(lower_b, lower_b.T)
    chol2 = jnp.linalg.cholesky(update)
    inv2 = jax.scipy.linalg.solve_triangular(chol2, identity, lower=True)
    remain = schur[:, half:] - matmul(lcol1, lower_b.T)
    lcol2 = matmul(remain, inv2.T)
    own_two = lax.dynamic_slice_in_dim(chol2, jnp.clip(first - half, 0, half - rows), rows, 0)
    lcol2 = jnp.where(first < width, own_two, lcol2)
    lcol2 = jnp.where(first < half, jnp.zeros_like(lcol2), lcol2)
    return jnp.concatenate([lcol1, lcol2], axis=1)


F32 = jnp.float32
BF16 = jnp.bfloat16
STEPS = 3
SETTLED = 1.6e-5


def split(x):
    high = x.astype(BF16)
    return high, (x - high.astype(F32)).astype(BF16)


def dot(a, b, contract=((1,), (0,))):
    return lax.dot_general(a, b, (contract, ((), ())), preferred_element_type=F32)


def dot3(a, b, contract=((1,), (0,))):
    (a_high, a_low), (b_high, b_low) = a, b
    return (
        dot(a_high, b_high, contract) + dot(a_high, b_low, contract) + dot(a_low, b_high, contract)
    )


NT = ((1,), (1,))


def kernel(
    n_scen,
    n_col,
    quarter,
    sub,
    lag,
    inv_hbm,
    coup_hbm,
    mask_ref,
    hess_ref,
    out_ref,
    flag_ref,
    inv,
    coup,
    high_t,
    low_t,
    prod,
    prod_high,
    prod_low,
    contrib,
    pair_slots,
    slots,
    plane_own,
    plane_pair,
    plane_slots,
    corner,
    scaled_high,
    scaled_low,
    y,
    y_next,
    y_high,
    y_low,
    y_out,
    late_out,
    load_sem,
    ring_send,
    ring_recv,
    pair_send,
    pair_recv,
    sum_send,
    sum_recv,
    plane_pair_send,
    plane_pair_recv,
    plane_send,
    plane_recv,
    fill_send,
    fill_recv,
    fill_pair_send,
    fill_pair_recv,
    y_send,
    y_recv,
    late_send,
    late_recv,
):
    me = lax.axis_index("scen")
    z = lax.axis_index("col")
    depth = coup.shape[0]
    block = coup.shape[1]
    width = corner.shape[3]
    chunk = prod.shape[2]
    n_chunk = prod.shape[0]
    rows = block // n_scen
    piece = width // n_scen
    owners = width // rows
    tile = depth // mask_ref.shape[1]
    half = depth // 2
    n_sub = half // sub
    nb = width // 2
    n_chip = n_scen // 2
    chip = me // 2
    core = lax.rem(me, 2)
    other = 1 - core
    partner = chip * 2 + other

    barrier = pltpu.get_barrier_semaphore()

    coup_panel = pltpu.make_async_copy(
        coup_hbm.at[0, :, pl.ds(0, width)], coup.at[:, pl.ds(0, width)], load_sem.at[0]
    )
    coup_rest = pltpu.make_async_copy(
        coup_hbm.at[0, :, pl.ds(width, block - width)],
        coup.at[:, pl.ds(width, block - width)],
        load_sem.at[1],
    )
    inv_load = pltpu.make_async_copy(inv_hbm.at[0], inv, load_sem.at[2])
    coup_panel.start()

    @pl.when(z == 0)
    def _():
        inv_load.start()

    coup_rest.start()

    def greet_scen(k, _):
        pl.semaphore_signal(
            barrier,
            inc=1,
            device_id={"scen": lax.rem(me + k, n_scen)},
            device_id_type=pl.DeviceIdType.MESH,
        )
        return 0

    def greet_col(k, _):
        pl.semaphore_signal(
            barrier,
            inc=1,
            device_id={"col": lax.rem(z + k, n_col)},
            device_id_type=pl.DeviceIdType.MESH,
        )
        return 0

    lax.fori_loop(1, n_scen, greet_scen, 0)
    lax.fori_loop(1, n_col, greet_col, 0)
    pl.semaphore_wait(barrier, n_scen + n_col - 2)

    def ring_copy(way, g):
        s = lax.rem(g, n_sub)
        at = prod.at[g // n_sub, pl.ds(pl.multiple_of(way * half + s * sub, sub), sub), :]
        to = lax.rem(z + 1, n_col) if way == 0 else lax.rem(z + n_col - 1, n_col)
        return pltpu.make_async_remote_copy(
            src_ref=at,
            dst_ref=at,
            send_sem=ring_send.at[way, g],
            recv_sem=ring_recv.at[way, g],
            device_id={"col": to},
            device_id_type=pl.DeviceIdType.MESH,
        )

    def transpose_coupling(first, count):
        @pl.loop(0, depth // 128)
        def _(t):
            at = pl.ds(pl.multiple_of(t * 128, 128), 128)
            high, low = split(coup[at, pl.ds(first, count)].T)
            high_t[pl.ds(first, count), at] = high
            low_t[pl.ds(first, count), at] = low

    def split_prod(q):
        high, low = split(prod[q])
        prod_high[...] = high
        prod_low[...] = low

    per = quarter // rows // 2

    def pair_copy(q, r):
        at = pl.ds(pl.multiple_of(r * per, per), per)
        return pltpu.make_async_remote_copy(
            src_ref=contrib.at[q, at, other],
            dst_ref=pair_slots.at[q, at],
            send_sem=pair_send.at[q],
            recv_sem=pair_recv.at[q, r],
            device_id={"scen": partner},
            device_id_type=pl.DeviceIdType.MESH,
        )

    def form(q, r):
        at = pl.ds(pl.multiple_of(r * quarter, quarter), quarter)
        term = dot3((high_t[at, :], low_t[at, :]), (prod_high[...], prod_low[...]))
        contrib[q, pl.ds(pl.multiple_of(r * per, per), per)] = term.reshape(per, 2, rows, chunk)
        pair_copy(q, r).start()

    def pass_on(q, r):
        pair_copy(q, r).wait_recv()
        at = pl.ds(pl.multiple_of(r * per, per), per)
        contrib[q, at, core] = contrib[q, at, core] + pair_slots[q, at]

        def start(k, _):
            to = lax.rem(chip + k, per) + r * per

            @pl.when(to != chip)
            def _():
                pltpu.make_async_remote_copy(
                    src_ref=contrib.at[q, to, core],
                    dst_ref=slots.at[q, lax.rem(chip - to + n_chip, n_chip) - 1],
                    send_sem=sum_send.at[q],
                    recv_sem=sum_recv.at[q],
                    device_id={"scen": to * 2 + core},
                    device_id_type=pl.DeviceIdType.MESH,
                ).start()

            return 0

        lax.fori_loop(0, per, start, 0)

    def own_rows(q):
        own = contrib[q, chip, core]
        return lax.fori_loop(0, n_chip - 1, lambda k, total: total + slots[q, k], own)

    def y_copy(to):
        return pltpu.make_async_remote_copy(
            src_ref=y_out,
            dst_ref=corner.at[chip, core],
            send_sem=y_send,
            recv_sem=y_recv,
            device_id={"col": to},
            device_id_type=pl.DeviceIdType.MESH,
        )

    def fill_copy(k):
        return pltpu.make_async_remote_copy(
            src_ref=corner.at[chip, core],
            dst_ref=corner.at[chip, core],
            send_sem=fill_send,
            recv_sem=fill_recv.at[n_chip - 1 - k],
            device_id={"scen": lax.rem(chip + k, n_chip) * 2 + core},
            device_id_type=pl.DeviceIdType.MESH,
        )

    def hand_copy(k, which):
        at = corner.at[lax.rem(chip + k, n_chip), which]
        return pltpu.make_async_remote_copy(
            src_ref=at,
            dst_ref=at,
            send_sem=fill_pair_send,
            recv_sem=fill_pair_recv.at[k],
            device_id={"scen": partner},
            device_id_type=pl.DeviceIdType.MESH,
        )

    def fill_start(k, _):
        fill_copy(k).start()
        return 0

    def fill_begin():
        hand_copy(0, core).start()
        lax.fori_loop(1, n_chip, fill_start, 0)

    def fill_hand(k, _):
        theirs = corner.at[lax.rem(chip + k, n_chip), core]
        pltpu.make_async_copy(theirs, theirs, fill_recv.at[k - 1]).wait()
        hand_copy(k, core).start()
        return 0

    def hand_wait(k, _):
        hand_copy(k, other).wait_recv()
        return 0

    def fill_end():
        lax.fori_loop(1, n_chip, fill_hand, 0)
        lax.fori_loop(0, n_chip, hand_wait, 0)

    def fill_drain():
        some = corner.at[pl.ds(1, n_chip - 1), 0]
        pltpu.make_async_copy(some, some, fill_send).wait()
        some = corner.at[:, 0]
        pltpu.make_async_copy(some, some, fill_pair_send).wait()
    @pl.when(z == 0)
    def _():
        coup_panel.wait()
        inv_load.wait()
        keep = jnp.concatenate(
            [
                jnp.full((tile, 1), mask_ref[0, t], jnp.int32).astype(F32)
                for t in range(mask_ref.shape[1])
            ],
            axis=0,
        )

        for q in range(n_chunk):
            panel = split(coup[:, pl.ds(q * chunk, chunk)] * keep)
            for r in range(depth // quarter):
                n_half = half // quarter
                r = (r % 2) * n_half + r // 2
                kept = inv[pl.ds(r * quarter, quarter), :]
                scale = keep[r * quarter : (r + 1) * quarter]
                prod[q, pl.ds(r * quarter, quarter), :] = dot3(split(kept), panel) * scale
                way = r // n_half
                for s in range(quarter // sub):
                    ring_copy(way, q * n_sub + (r % n_half) * (quarter // sub) + s).start()

        def plane_pair_copy(part):
            return pltpu.make_async_remote_copy(
                src_ref=plane_own.at[part, :, other],
                dst_ref=plane_pair.at[part],
                send_sem=plane_pair_send.at[part],
                recv_sem=plane_pair_recv.at[part],
                device_id={"scen": partner},
                device_id_type=pl.DeviceIdType.MESH,
            )

        def plane_form(part):
            group = quarter // piece // 2
            for q in range(n_chunk):
                split_prod(q)
                for r in range(width // quarter):
                    at = pl.ds(part * width + r * quarter, quarter)
                    term = dot3((high_t[at, :], low_t[at, :]), (prod_high[...], prod_low[...]))
                    plane_own[part, pl.ds(r * group, group), :, :, pl.ds(q * chunk, chunk)] = (
                        term.reshape(group, 2, piece, chunk)
                    )
            plane_pair_copy(part).start()

        def plane_pass_on(part):
            plane_pair_copy(part).wait_recv()
            step = max(1, n_chip // 4)
            for r in range(0, n_chip, step):
                at = pl.ds(r, step)
                plane_own[part, at, core] = plane_own[part, at, core] + plane_pair[part, at]

            def start(k, _):
                to = lax.rem(chip + k, n_chip)
                pltpu.make_async_remote_copy(
                    src_ref=plane_own.at[part, to, core],
                    dst_ref=plane_slots.at[part, n_chip - 1 - k],
                    send_sem=plane_send.at[part],
                    recv_sem=plane_recv.at[part],
                    device_id={"scen": to * 2 + core},
                    device_id_type=pl.DeviceIdType.MESH,
                ).start()
                return 0

            lax.fori_loop(1, n_chip, start, 0)

        def plane_total(part):
            some = plane_slots.at[part]
            pltpu.make_async_copy(some, some, plane_recv.at[part]).wait()
            return lax.fori_loop(
                0,
                n_chip - 1,
                lambda k, total: total + plane_slots[part, k],
                plane_own[part, chip, core],
            )

        transpose_coupling(0, width)
        plane_form(0)
        coup_rest.wait()
        transpose_coupling(width, block - width)
        plane_pass_on(0)
        plane_form(1)
        total = plane_total(0)
        row = me * piece + lax.broadcasted_iota(jnp.int32, (piece, width), 0)
        column = lax.broadcasted_iota(jnp.int32, (piece, width), 1)
        corner[chip, core] = total + jnp.where(row == column, hess_ref[...], 0.0)

        fill_begin()
        fill_end()
        plane_pass_on(1)

        row = lax.broadcasted_iota(jnp.int32, (width, width), 0)
        column = lax.broadcasted_iota(jnp.int32, (width, width), 1)
        whole = corner[...].reshape(width, width)
        on_diagonal = jnp.where(row == column, whole, 0.0)
        root_row = lax.rsqrt(jnp.sum(on_diagonal, axis=0, keepdims=True))
        root_column = lax.rsqrt(jnp.sum(on_diagonal, axis=1, keepdims=True))
        scaled = whole * root_column * root_row
        high, low = split(scaled)
        scaled_high[...] = high
        scaled_low[...] = low
        y[...] = jnp.where(row == column, 1.0, jnp.where(row > column, -scaled, 0.0))

        for step in range(STEPS):
            high, low = split(y[...])
            y_high[...] = high
            y_low[...] = low
            size = jnp.zeros((1, 1), F32)
            for r in range(2):
                at = pl.ds(r * nb, nb)
                to = pl.ds(0, (r + 1) * nb)
                t = dot3((y_high[at, to], y_low[at, to]), (scaled_high[to, to], scaled_low[to, to]))
                e = dot3(split(t), (y_high[to, to], y_low[to, to]), NT)
                e_row = r * nb + lax.broadcasted_iota(jnp.int32, e.shape, 0)
                e_column = lax.broadcasted_iota(jnp.int32, e.shape, 1)
                e = jnp.where(e_row == e_column, e - 1.0, jnp.where(e_row > e_column, e, 0.0))
                if step == STEPS - 1:
                    size = size + jnp.sum(e * e, keepdims=True)
                e = jnp.where(e_row == e_column, 0.5 * e, e)
                y_next[at, to] = y[at, to] - dot3(split(e), (y_high[to, to], y_low[to, to]))
            for r in range(2):
                at = pl.ds(r * nb, nb)
                to = pl.ds(0, (r + 1) * nb)
                y[at, to] = y_next[at, to]

        bad = jnp.where(size < SETTLED, 0.0, 1.0)
        y[...] = jnp.where(bad > 0.5, jnp.nan, y[...] * root_row)
        y_out[...] = y[pl.ds(pl.multiple_of(me * piece, piece), piece), :]

        def y_start(k, _):
            y_copy(n_col // 2 + (k // 2) * (1 - 2 * lax.rem(k, 2))).start()
            return 0

        lax.fori_loop(1, n_col, y_start, 0)
        y_final = split(y[...])

        later = plane_total(1)
        late_out[1, 0] = dot3(split(later), y_final, NT)
        late_to = owners + me * piece // rows
        late_part = lax.rem(me, rows // piece)

        def late_copy():
            return pltpu.make_async_remote_copy(
                src_ref=late_out.at[1, 0],
                dst_ref=late_out.at[0, late_part],
                send_sem=late_send,
                recv_sem=late_recv.at[late_part],
                device_id={"scen": late_to},
                device_id_type=pl.DeviceIdType.MESH,
            )

        @pl.when(late_to != me)
        def _():
            late_copy().start()

        @pl.when(me < owners)
        def _():
            chips = rows // piece // 2
            given = corner[pl.ds(lax.rem(me, owners) * chips, chips)].reshape(rows, width)
            row = me * rows + lax.broadcasted_iota(jnp.int32, (rows, width), 0)
            column = lax.broadcasted_iota(jnp.int32, (rows, width), 1)
            solved = dot3(split(given), y_final, NT)
            out_ref[...] = jnp.where(column <= row, solved, 0.0)

        @pl.when(me >= owners)
        def _():
            for part in range(rows // piece):

                @pl.when(jnp.logical_and(late_to == me, late_part == part))
                def _():
                    out_ref[pl.ds(part * piece, piece), :] = late_out[1, 0]

                @pl.when(jnp.logical_not(jnp.logical_and(late_to == me, late_part == part)))
                def _():
                    some = late_out.at[0, part]
                    pltpu.make_async_copy(some, some, late_recv.at[part]).wait()
                    out_ref[pl.ds(part * piece, piece), :] = late_out[0, part]

        flag_ref[...] = jnp.broadcast_to(bad, flag_ref.shape)

        @pl.loop(0, n_chunk * n_sub)
        def _(g):
            ring_copy(0, g).wait_send()
            ring_copy(1, g).wait_send()

        for part in range(2):
            plane_pair_copy(part).wait_send()
            some = plane_slots.at[part]
            pltpu.make_async_copy(some, some, plane_send.at[part]).wait()
        fill_drain()

        @pl.when(late_to != me)
        def _():
            late_copy().wait_send()

        def y_wait(k, _):
            y_copy(k).wait_send()
            return 0

        lax.fori_loop(1, n_col, y_wait, 0)

    @pl.when(z != 0)
    def _():
        coup_panel.wait()
        coup_rest.wait()
        transpose_coupling(0, block)

        late = lag * jnp.maximum(z - 1, n_col - 1 - z)
        n_piece = n_chunk * n_sub
        n_row = block // quarter

        @pl.loop(0, n_piece + late)
        def _(t):
            g = t - lag * (z - 1)

            @pl.when(jnp.logical_and(g >= 0, g < n_piece))
            def _():
                up = ring_copy(0, g)
                up.wait_recv()

                @pl.when(z < n_col - 1)
                def _():
                    up.start()

            h = t - lag * (n_col - 1 - z)

            @pl.when(jnp.logical_and(h >= 0, h < n_piece))
            def _():
                down = ring_copy(1, h)
                down.wait_recv()

                @pl.when(z > 1)
                def _():
                    down.start()

            done = t - late + 1
            q = done // n_sub - 1
            r = lax.rem(done, n_sub)
            whole = done >= n_sub

            @pl.when(jnp.logical_and(whole, r == 0))
            def _():
                split_prod(q)

            inside = jnp.logical_and(whole, done < n_piece)

            @pl.when(jnp.logical_and(inside, r < n_row))
            def _():
                form(q, r)

            @pl.when(jnp.logical_and(inside, jnp.logical_and(r >= 1, r <= n_row)))
            def _():
                pass_on(q, r - 1)

        form(n_chunk - 1, 0)

        @pl.loop(1, n_row)
        def _(r):
            form(n_chunk - 1, r)
            pass_on(n_chunk - 1, r - 1)

        pass_on(n_chunk - 1, n_row - 1)

        y_copy(0).wait_recv()
        fill_begin()
        given = []
        for q in range(n_chunk):
            pltpu.make_async_copy(slots.at[q], slots.at[q], sum_recv.at[q]).wait()
            given.append(own_rows(q))
        given = split(jnp.concatenate(given, axis=1))
        fill_end()
        factor = corner[...].reshape(width, width)
        out_ref[...] = dot3(given, split(factor), NT)
        last = factor[width - 1 :, width - 1 :]
        flag_ref[...] = jnp.broadcast_to(jnp.where(last == last, 0.0, 1.0), flag_ref.shape)

        fill_drain()
        for q in range(n_chunk):
            pltpu.make_async_copy(slots.at[q], slots.at[q], sum_send.at[q]).wait()
            pltpu.make_async_copy(pair_slots.at[q], pair_slots.at[q], pair_send.at[q]).wait()

        @pl.loop(0, n_piece)
        def _(g):
            @pl.when(z < n_col - 1)
            def _():
                ring_copy(0, g).wait_send()

            @pl.when(z > 1)
            def _():
                ring_copy(1, g).wait_send()


def fused(inverses, coupling, tile_mask, hess_diag, quarter=256, chunk=128, sub=64, lag=5):
    n_scen = lax.axis_size("scen")
    n_col = lax.axis_size("col")
    _, depth, block = coupling.shape
    width = hess_diag.shape[0]
    rows = block // n_scen
    piece = width // n_scen
    n_chunk = width // chunk
    n_sub = depth // 2 // sub
    vmem = pltpu.VMEM
    dma = pltpu.SemaphoreType.DMA
    scratch = [
        vmem((depth, depth), F32),
        vmem((depth, block), F32),
        vmem((block, depth), BF16),
        vmem((block, depth), BF16),
        vmem((n_chunk, depth, chunk), F32),
        vmem((depth, chunk), BF16),
        vmem((depth, chunk), BF16),
        vmem((n_chunk, n_scen // 2, 2, rows, chunk), F32),
        vmem((n_chunk, n_scen // 2, rows, chunk), F32),
        vmem((n_chunk, n_scen // 2 - 1, rows, chunk), F32),
        vmem((2, n_scen // 2, 2, piece, width), F32),
        vmem((2, n_scen // 2, piece, width), F32),
        vmem((2, n_scen // 2 - 1, piece, width), F32),
        vmem((n_scen // 2, 2, piece, width), F32),
        vmem((width, width), BF16),
        vmem((width, width), BF16),
        vmem((width, width), F32),
        vmem((width, width), F32),
        vmem((width, width), BF16),
        vmem((width, width), BF16),
        vmem((piece, width), F32),
        vmem((2, rows // piece, piece, width), F32),
        dma((3,)),
        dma((2, n_chunk * n_sub)),
        dma((2, n_chunk * n_sub)),
        dma((n_chunk,)),
        dma((n_chunk, block // quarter)),
        dma((n_chunk,)),
        dma((n_chunk,)),
        dma((2,)),
        dma((2,)),
        dma((2,)),
        dma((2,)),
        dma(()),
        dma((n_scen // 2 - 1,)),
        dma(()),
        dma((n_scen // 2,)),
        dma(()),
        dma(()),
        dma(()),
        dma((rows // piece,)),
    ]
    return pl.pallas_call(
        functools.partial(kernel, n_scen, n_col, quarter, sub, lag),
        out_shape=(
            jax.ShapeDtypeStruct((rows, width), F32),
            jax.ShapeDtypeStruct((8, 128), F32),
        ),
        in_specs=[
            pl.BlockSpec(memory_space=pl.ANY),
            pl.BlockSpec(memory_space=pl.ANY),
            pl.BlockSpec(memory_space=pltpu.SMEM),
            pl.BlockSpec(memory_space=pltpu.VMEM),
        ],
        out_specs=[pl.BlockSpec(memory_space=pltpu.VMEM)] * 2,
        scratch_shapes=scratch,
        compiler_params=pltpu.CompilerParams(
            collective_id=0, has_side_effects=True, vmem_limit_bytes=50 * 2**20
        ),
    )(inverses, coupling, tile_mask, hess_diag[None, :])


def body(inverses, coupling, tile_mask, hess_diag):
    factor, flag = fused(inverses, coupling, tile_mask, hess_diag)
    return lax.cond(
        flag[0, 0] > 0.5,
        direct_body,
        lambda *_: factor,
        inverses,
        coupling,
        tile_mask,
        hess_diag,
    )


def solution(mesh):
    in_specs = (P("scen", None, None), P("scen", None, "col"), P("scen", None), P())
    out_specs = P(("col", "scen"), None)
    return jax.shard_map(body, mesh=mesh, in_specs=in_specs, out_specs=out_specs, check_vma=False)
```

```python
import functools

import jax
import jax.numpy as jnp
from jax import lax
from jax.experimental import pallas as pl
from jax.experimental.pallas import tpu as pltpu
from jax.sharding import PartitionSpec as P


def from_first(x, axis):
    at = lax.axis_index(axis)
    have = 1
    while have < lax.axis_size(axis):
        pairs = [(i, i + have) for i in range(min(have, lax.axis_size(axis) - have))]
        got = lax.ppermute(x, axis, pairs)
        x = jnp.where(jnp.logical_and(at >= have, at < 2 * have), got, x)
        have *= 2
    return x


def in_blocks(x, dim, size):
    lengths = x.shape
    blocks = x.reshape(*lengths[:dim], size, lengths[dim] // size, *lengths[dim + 1 :])
    return jnp.moveaxis(blocks, dim, 0)


def sum_at_owner(x, axis, dim):
    size = lax.axis_size(axis)
    blocks = lax.all_to_all(in_blocks(x, dim, size), axis, 0, 0, tiled=True)
    return jnp.sum(blocks, axis=0)


def sent_to_all(x, axis):
    size = lax.axis_size(axis)
    return lax.all_to_all(jnp.broadcast_to(x[None], (size, *x.shape)), axis, 0, 0, tiled=True)


def in_order(blocks, dim):
    lengths = list(blocks.shape[1:])
    lengths[dim] *= blocks.shape[0]
    return jnp.moveaxis(blocks, 0, dim).reshape(lengths)


def collect(x, axis, dim):
    blocks = sent_to_all(x, axis)
    return in_order(blocks, dim)


def outer_rows(left, piece):
    return lax.dot_general(
        left,
        piece,
        (((0,), (0,)), ((), ())),
        precision=lax.Precision.HIGHEST,
        preferred_element_type=jnp.float32,
    )


def matmul(left, right):
    return jnp.dot(left, right, precision=lax.Precision.HIGHEST, preferred_element_type=jnp.float32)


def direct_body(inverses, coupling, tile_mask, hess_diag):
    inverse = inverses[0]
    local = coupling[0]
    width = hess_diag.shape[0]
    half = width // 2
    scen_size = lax.axis_size("scen")
    rows = local.shape[1] // scen_size
    row_keep = jnp.repeat(tile_mask[0].astype(jnp.float32), local.shape[0] // tile_mask.shape[1])
    panel = from_first(local[:, :width], "col")
    panel = panel * row_keep[:, None]
    product = matmul(inverse, panel) * row_keep[:, None]
    block = local
    summed = sum_at_owner(outer_rows(block, product), "scen", 0)
    first = lax.axis_index("col") * local.shape[1] + lax.axis_index("scen") * rows
    global_rows = first + jnp.arange(rows, dtype=jnp.int32)
    columns = jnp.arange(width, dtype=jnp.int32)
    schur = summed + jnp.where(columns[None, :] == global_rows[:, None], hess_diag[None, :], 0.0)

    def fetch(stacked, low):
        whole = collect(stacked, "scen", 1)
        block = whole[:, low : low + half]
        return from_first(block, "col")

    identity = jnp.eye(half, dtype=jnp.float32)
    block_one = fetch(schur[None, :, :half], 0)[0]
    chol1 = jnp.linalg.cholesky(block_one)
    inv1 = jax.scipy.linalg.solve_triangular(chol1, identity, lower=True)
    lcol1 = matmul(schur[:, :half], inv1.T)
    own_one = lax.dynamic_slice_in_dim(chol1, jnp.clip(first, 0, half - rows), rows, 0)
    lcol1 = jnp.where(first < half, own_one, lcol1)
    paired = fetch(jnp.stack([schur[:, half:], lcol1]), half)
    lower_b = paired[1]
    update = paired[0] - matmul(lower_b, lower_b.T)
    chol2 = jnp.linalg.cholesky(update)
    inv2 = jax.scipy.linalg.solve_triangular(chol2, identity, lower=True)
    remain = schur[:, half:] - matmul(lcol1, lower_b.T)
    lcol2 = matmul(remain, inv2.T)
    own_two = lax.dynamic_slice_in_dim(chol2, jnp.clip(first - half, 0, half - rows), rows, 0)
    lcol2 = jnp.where(first < width, own_two, lcol2)
    lcol2 = jnp.where(first < half, jnp.zeros_like(lcol2), lcol2)
    return jnp.concatenate([lcol1, lcol2], axis=1)


F32 = jnp.float32
BF16 = jnp.bfloat16
STEPS = 3
SETTLED = 1.6e-5


def split(x):
    high = x.astype(BF16)
    return high, (x - high.astype(F32)).astype(BF16)


def dot(a, b, contract=((1,), (0,))):
    return lax.dot_general(a, b, (contract, ((), ())), preferred_element_type=F32)


def dot3(a, b, contract=((1,), (0,))):
    (a_high, a_low), (b_high, b_low) = a, b
    return (
        dot(a_high, b_high, contract) + dot(a_high, b_low, contract) + dot(a_low, b_high, contract)
    )


NT = ((1,), (1,))


def kernel(
    n_scen,
    n_col,
    quarter,
    sub,
    lag,
    inv_hbm,
    coup_hbm,
    mask_ref,
    hess_ref,
    out_ref,
    flag_ref,
    inv,
    coup,
    high_t,
    low_t,
    prod,
    prod_high,
    prod_low,
    contrib,
    pair_slots,
    slots,
    plane_own,
    plane_pair,
    plane_slots,
    corner,
    scaled_high,
    scaled_low,
    y,
    y_next,
    y_high,
    y_low,
    y_out,
    late_out,
    load_sem,
    ring_send,
    ring_recv,
    pair_send,
    pair_recv,
    sum_send,
    sum_recv,
    plane_pair_send,
    plane_pair_recv,
    plane_send,
    plane_recv,
    fill_send,
    fill_recv,
    fill_pair_send,
    fill_pair_recv,
    y_send,
    y_recv,
    late_send,
    late_recv,
):
    me = lax.axis_index("scen")
    z = lax.axis_index("col")
    depth = coup.shape[0]
    block = coup.shape[1]
    width = corner.shape[3]
    chunk = prod.shape[2]
    n_chunk = prod.shape[0]
    rows = block // n_scen
    piece = width // n_scen
    owners = width // rows
    tile = depth // mask_ref.shape[1]
    half = depth // 2
    n_sub = half // sub
    nb = width // 2
    n_chip = n_scen // 2
    chip = me // 2
    core = lax.rem(me, 2)
    other = 1 - core
    partner = chip * 2 + other

    barrier = pltpu.get_barrier_semaphore()

    coup_panel = pltpu.make_async_copy(
        coup_hbm.at[0, :, pl.ds(0, width)], coup.at[:, pl.ds(0, width)], load_sem.at[0]
    )
    coup_rest = pltpu.make_async_copy(
        coup_hbm.at[0, :, pl.ds(width, block - width)],
        coup.at[:, pl.ds(width, block - width)],
        load_sem.at[1],
    )
    inv_load = pltpu.make_async_copy(inv_hbm.at[0], inv, load_sem.at[2])
    coup_panel.start()

    @pl.when(z == 0)
    def _():
        inv_load.start()

    coup_rest.start()

    def greet_scen(k, _):
        pl.semaphore_signal(
            barrier,
            inc=1,
            device_id={"scen": lax.rem(me + k, n_scen)},
            device_id_type=pl.DeviceIdType.MESH,
        )
        return 0

    def greet_col(k, _):
        pl.semaphore_signal(
            barrier,
            inc=1,
            device_id={"col": lax.rem(z + k, n_col)},
            device_id_type=pl.DeviceIdType.MESH,
        )
        return 0

    lax.fori_loop(1, n_scen, greet_scen, 0)
    lax.fori_loop(1, n_col, greet_col, 0)
    pl.semaphore_wait(barrier, n_scen + n_col - 2)

    n_piece = n_chunk * n_sub
    common = n_piece - n_sub
    entries = n_piece + n_sub
    mid = n_col // 2

    def ring_copy(way, e):
        over = jnp.maximum(e - common, 0)
        g = jnp.minimum(e, common) + over // 2
        part = lax.rem(way + lax.rem(over, 2), 2)
        s = lax.rem(g, n_sub)
        at = prod.at[g // n_sub, pl.ds(pl.multiple_of(part * half + s * sub, sub), sub), :]
        to = lax.rem(z + 1, n_col) if way == 0 else lax.rem(z + n_col - 1, n_col)
        return pltpu.make_async_remote_copy(
            src_ref=at,
            dst_ref=at,
            send_sem=ring_send.at[way, e],
            recv_sem=ring_recv.at[way, e],
            device_id={"col": to},
            device_id_type=pl.DeviceIdType.MESH,
        )

    def transpose_coupling(first, count):
        @pl.loop(0, depth // 128)
        def _(t):
            at = pl.ds(pl.multiple_of(t * 128, 128), 128)
            high, low = split(coup[at, pl.ds(first, count)].T)
            high_t[pl.ds(first, count), at] = high
            low_t[pl.ds(first, count), at] = low

    def split_prod(q):
        high, low = split(prod[q])
        prod_high[...] = high
        prod_low[...] = low

    per = quarter // rows // 2

    def pair_copy(q, r):
        at = pl.ds(pl.multiple_of(r * per, per), per)
        return pltpu.make_async_remote_copy(
            src_ref=contrib.at[q, at, other],
            dst_ref=pair_slots.at[q, at],
            send_sem=pair_send.at[q],
            recv_sem=pair_recv.at[q, r],
            device_id={"scen": partner},
            device_id_type=pl.DeviceIdType.MESH,
        )

    def form(q, r):
        at = pl.ds(pl.multiple_of(r * quarter, quarter), quarter)
        term = dot3((high_t[at, :], low_t[at, :]), (prod_high[...], prod_low[...]))
        contrib[q, pl.ds(pl.multiple_of(r * per, per), per)] = term.reshape(per, 2, rows, chunk)
        pair_copy(q, r).start()

    def pass_on(q, r):
        pair_copy(q, r).wait_recv()
        at = pl.ds(pl.multiple_of(r * per, per), per)
        contrib[q, at, core] = contrib[q, at, core] + pair_slots[q, at]

        def start(k, _):
            to = lax.rem(chip + k, per) + r * per

            @pl.when(to != chip)
            def _():
                pltpu.make_async_remote_copy(
                    src_ref=contrib.at[q, to, core],
                    dst_ref=slots.at[q, lax.rem(chip - to + n_chip, n_chip) - 1],
                    send_sem=sum_send.at[q],
                    recv_sem=sum_recv.at[q],
                    device_id={"scen": to * 2 + core},
                    device_id_type=pl.DeviceIdType.MESH,
                ).start()

            return 0

        lax.fori_loop(0, per, start, 0)

    def own_rows(q):
        own = contrib[q, chip, core]
        return lax.fori_loop(0, n_chip - 1, lambda k, total: total + slots[q, k], own)

    def y_copy(to):
        return pltpu.make_async_remote_copy(
            src_ref=y_out,
            dst_ref=corner.at[chip, core],
            send_sem=y_send,
            recv_sem=y_recv,
            device_id={"col": to},
            device_id_type=pl.DeviceIdType.MESH,
        )

    def fill_copy(k):
        return pltpu.make_async_remote_copy(
            src_ref=corner.at[chip, core],
            dst_ref=corner.at[chip, core],
            send_sem=fill_send,
            recv_sem=fill_recv.at[n_chip - 1 - k],
            device_id={"scen": lax.rem(chip + k, n_chip) * 2 + core},
            device_id_type=pl.DeviceIdType.MESH,
        )

    def hand_copy(k, which):
        at = corner.at[lax.rem(chip + k, n_chip), which]
        return pltpu.make_async_remote_copy(
            src_ref=at,
            dst_ref=at,
            send_sem=fill_pair_send,
            recv_sem=fill_pair_recv.at[k],
            device_id={"scen": partner},
            device_id_type=pl.DeviceIdType.MESH,
        )

    def fill_start(k, _):
        fill_copy(k).start()
        return 0

    def fill_begin():
        hand_copy(0, core).start()
        lax.fori_loop(1, n_chip, fill_start, 0)

    def fill_hand(k, _):
        theirs = corner.at[lax.rem(chip + k, n_chip), core]
        pltpu.make_async_copy(theirs, theirs, fill_recv.at[k - 1]).wait()
        hand_copy(k, core).start()
        return 0

    def hand_wait(k, _):
        hand_copy(k, other).wait_recv()
        return 0

    def fill_end():
        lax.fori_loop(1, n_chip, fill_hand, 0)
        lax.fori_loop(0, n_chip, hand_wait, 0)

    def fill_drain():
        some = corner.at[pl.ds(1, n_chip - 1), 0]
        pltpu.make_async_copy(some, some, fill_send).wait()
        some = corner.at[:, 0]
        pltpu.make_async_copy(some, some, fill_pair_send).wait()
    @pl.when(z == 0)
    def _():
        coup_panel.wait()
        inv_load.wait()
        keep = jnp.concatenate(
            [
                jnp.full((tile, 1), mask_ref[0, t], jnp.int32).astype(F32)
                for t in range(mask_ref.shape[1])
            ],
            axis=0,
        )

        for q in range(n_chunk):
            panel = split(coup[:, pl.ds(q * chunk, chunk)] * keep)
            for r in range(depth // quarter):
                n_half = half // quarter
                r = (r % 2) * n_half + r // 2
                kept = inv[pl.ds(r * quarter, quarter), :]
                scale = keep[r * quarter : (r + 1) * quarter]
                prod[q, pl.ds(r * quarter, quarter), :] = dot3(split(kept), panel) * scale
                way = r // n_half
                for s in range(quarter // sub):
                    g = q * n_sub + (r % n_half) * (quarter // sub) + s
                    if g < common:
                        ring_copy(way, g).start()
                    else:
                        ring_copy(way, 2 * g - common).start()
                        ring_copy(1 - way, 2 * g - common + 1).start()

        def plane_pair_copy(part):
            return pltpu.make_async_remote_copy(
                src_ref=plane_own.at[part, :, other],
                dst_ref=plane_pair.at[part],
                send_sem=plane_pair_send.at[part],
                recv_sem=plane_pair_recv.at[part],
                device_id={"scen": partner},
                device_id_type=pl.DeviceIdType.MESH,
            )

        def plane_form(part):
            group = quarter // piece // 2
            for q in range(n_chunk):
                split_prod(q)
                for r in range(width // quarter):
                    at = pl.ds(part * width + r * quarter, quarter)
                    term = dot3((high_t[at, :], low_t[at, :]), (prod_high[...], prod_low[...]))
                    plane_own[part, pl.ds(r * group, group), :, :, pl.ds(q * chunk, chunk)] = (
                        term.reshape(group, 2, piece, chunk)
                    )
            plane_pair_copy(part).start()

        def plane_pass_on(part):
            plane_pair_copy(part).wait_recv()
            step = max(1, n_chip // 4)
            for r in range(0, n_chip, step):
                at = pl.ds(r, step)
                plane_own[part, at, core] = plane_own[part, at, core] + plane_pair[part, at]

            def start(k, _):
                to = lax.rem(chip + k, n_chip)
                pltpu.make_async_remote_copy(
                    src_ref=plane_own.at[part, to, core],
                    dst_ref=plane_slots.at[part, n_chip - 1 - k],
                    send_sem=plane_send.at[part],
                    recv_sem=plane_recv.at[part],
                    device_id={"scen": to * 2 + core},
                    device_id_type=pl.DeviceIdType.MESH,
                ).start()
                return 0

            lax.fori_loop(1, n_chip, start, 0)

        def plane_total(part):
            some = plane_slots.at[part]
            pltpu.make_async_copy(some, some, plane_recv.at[part]).wait()
            return lax.fori_loop(
                0,
                n_chip - 1,
                lambda k, total: total + plane_slots[part, k],
                plane_own[part, chip, core],
            )

        transpose_coupling(0, width)
        plane_form(0)
        coup_rest.wait()
        transpose_coupling(width, block - width)
        plane_pass_on(0)
        plane_form(1)
        total = plane_total(0)
        row = me * piece + lax.broadcasted_iota(jnp.int32, (piece, width), 0)
        column = lax.broadcasted_iota(jnp.int32, (piece, width), 1)
        corner[chip, core] = total + jnp.where(row == column, hess_ref[...], 0.0)

        fill_begin()
        fill_end()
        plane_pass_on(1)

        row = lax.broadcasted_iota(jnp.int32, (width, width), 0)
        column = lax.broadcasted_iota(jnp.int32, (width, width), 1)
        whole = corner[...].reshape(width, width)
        on_diagonal = jnp.where(row == column, whole, 0.0)
        root_row = lax.rsqrt(jnp.sum(on_diagonal, axis=0, keepdims=True))
        root_column = lax.rsqrt(jnp.sum(on_diagonal, axis=1, keepdims=True))
        scaled = whole * root_column * root_row
        high, low = split(scaled)
        scaled_high[...] = high
        scaled_low[...] = low
        y[...] = jnp.where(row == column, 1.0, jnp.where(row > column, -scaled, 0.0))

        for step in range(STEPS):
            high, low = split(y[...])
            y_high[...] = high
            y_low[...] = low
            size = jnp.zeros((1, 1), F32)
            for r in range(2):
                at = pl.ds(r * nb, nb)
                to = pl.ds(0, (r + 1) * nb)
                t = dot3((y_high[at, to], y_low[at, to]), (scaled_high[to, to], scaled_low[to, to]))
                e = dot3(split(t), (y_high[to, to], y_low[to, to]), NT)
                e_row = r * nb + lax.broadcasted_iota(jnp.int32, e.shape, 0)
                e_column = lax.broadcasted_iota(jnp.int32, e.shape, 1)
                e = jnp.where(e_row == e_column, e - 1.0, jnp.where(e_row > e_column, e, 0.0))
                if step == STEPS - 1:
                    size = size + jnp.sum(e * e, keepdims=True)
                e = jnp.where(e_row == e_column, 0.5 * e, e)
                y_next[at, to] = y[at, to] - dot3(split(e), (y_high[to, to], y_low[to, to]))
            for r in range(2):
                at = pl.ds(r * nb, nb)
                to = pl.ds(0, (r + 1) * nb)
                y[at, to] = y_next[at, to]

        bad = jnp.where(size < SETTLED, 0.0, 1.0)
        y[...] = jnp.where(bad > 0.5, jnp.nan, y[...] * root_row)
        y_out[...] = y[pl.ds(pl.multiple_of(me * piece, piece), piece), :]

        def y_start(k, _):
            y_copy(n_col // 2 + (k // 2) * (1 - 2 * lax.rem(k, 2))).start()
            return 0

        lax.fori_loop(1, n_col, y_start, 0)
        y_final = split(y[...])

        later = plane_total(1)
        late_out[1, 0] = dot3(split(later), y_final, NT)
        late_to = owners + me * piece // rows
        late_part = lax.rem(me, rows // piece)

        def late_copy():
            return pltpu.make_async_remote_copy(
                src_ref=late_out.at[1, 0],
                dst_ref=late_out.at[0, late_part],
                send_sem=late_send,
                recv_sem=late_recv.at[late_part],
                device_id={"scen": late_to},
                device_id_type=pl.DeviceIdType.MESH,
            )

        @pl.when(late_to != me)
        def _():
            late_copy().start()

        @pl.when(me < owners)
        def _():
            chips = rows // piece // 2
            given = corner[pl.ds(lax.rem(me, owners) * chips, chips)].reshape(rows, width)
            row = me * rows + lax.broadcasted_iota(jnp.int32, (rows, width), 0)
            column = lax.broadcasted_iota(jnp.int32, (rows, width), 1)
            solved = dot3(split(given), y_final, NT)
            out_ref[...] = jnp.where(column <= row, solved, 0.0)

        @pl.when(me >= owners)
        def _():
            for part in range(rows // piece):

                @pl.when(jnp.logical_and(late_to == me, late_part == part))
                def _():
                    out_ref[pl.ds(part * piece, piece), :] = late_out[1, 0]

                @pl.when(jnp.logical_not(jnp.logical_and(late_to == me, late_part == part)))
                def _():
                    some = late_out.at[0, part]
                    pltpu.make_async_copy(some, some, late_recv.at[part]).wait()
                    out_ref[pl.ds(part * piece, piece), :] = late_out[0, part]

        flag_ref[...] = jnp.broadcast_to(bad, flag_ref.shape)

        @pl.loop(0, entries)
        def _(g):
            ring_copy(0, g).wait_send()
            ring_copy(1, g).wait_send()

        for part in range(2):
            plane_pair_copy(part).wait_send()
            some = plane_slots.at[part]
            pltpu.make_async_copy(some, some, plane_send.at[part]).wait()
        fill_drain()

        @pl.when(late_to != me)
        def _():
            late_copy().wait_send()

        def y_wait(k, _):
            y_copy(k).wait_send()
            return 0

        lax.fori_loop(1, n_col, y_wait, 0)

    @pl.when(z != 0)
    def _():
        coup_panel.wait()
        coup_rest.wait()
        transpose_coupling(0, block)

        late = lag * jnp.maximum(z - 1, n_col - 1 - z)
        n_up = jnp.where(z <= mid, entries, common)
        n_down = jnp.where(z > mid, entries, common)
        steps = jnp.maximum(lag * (z - 1) + n_up, lag * (n_col - 1 - z) + n_down)
        n_row = block // quarter

        @pl.loop(0, jnp.maximum(n_piece + late, steps))
        def _(t):
            g = t - lag * (z - 1)

            @pl.when(jnp.logical_and(g >= 0, g < n_up))
            def _():
                up = ring_copy(0, g)
                up.wait_recv()

                @pl.when(z < jnp.where(g < common, n_col - 1, mid))
                def _():
                    up.start()

            h = t - lag * (n_col - 1 - z)

            @pl.when(jnp.logical_and(h >= 0, h < n_down))
            def _():
                down = ring_copy(1, h)
                down.wait_recv()

                @pl.when(z > jnp.where(h < common, 1, mid + 1))
                def _():
                    down.start()

            done = t - late + 1
            q = done // n_sub - 1
            r = lax.rem(done, n_sub)
            whole = done >= n_sub

            inside = jnp.logical_and(whole, done < n_piece)

            @pl.when(jnp.logical_and(inside, r == 0))
            def _():
                split_prod(q)

            @pl.when(jnp.logical_and(inside, r < n_row))
            def _():
                form(q, r)

            @pl.when(jnp.logical_and(inside, jnp.logical_and(r >= 1, r <= n_row)))
            def _():
                pass_on(q, r - 1)

        split_prod(n_chunk - 1)
        form(n_chunk - 1, 0)

        @pl.loop(1, n_row)
        def _(r):
            form(n_chunk - 1, r)
            pass_on(n_chunk - 1, r - 1)

        pass_on(n_chunk - 1, n_row - 1)

        y_copy(0).wait_recv()
        fill_begin()
        given = []
        for q in range(n_chunk):
            pltpu.make_async_copy(slots.at[q], slots.at[q], sum_recv.at[q]).wait()
            given.append(own_rows(q))
        given = split(jnp.concatenate(given, axis=1))
        fill_end()
        factor = corner[...].reshape(width, width)
        out_ref[...] = dot3(given, split(factor), NT)
        last = factor[width - 1 :, width - 1 :]
        flag_ref[...] = jnp.broadcast_to(jnp.where(last == last, 0.0, 1.0), flag_ref.shape)

        fill_drain()
        for q in range(n_chunk):
            pltpu.make_async_copy(slots.at[q], slots.at[q], sum_send.at[q]).wait()
            pltpu.make_async_copy(pair_slots.at[q], pair_slots.at[q], pair_send.at[q]).wait()

        @pl.loop(0, entries)
        def _(e):
            @pl.when(z < jnp.where(e < common, n_col - 1, mid))
            def _():
                ring_copy(0, e).wait_send()

            @pl.when(z > jnp.where(e < common, 1, mid + 1))
            def _():
                ring_copy(1, e).wait_send()


def fused(inverses, coupling, tile_mask, hess_diag, quarter=256, chunk=128, sub=64, lag=5):
    n_scen = lax.axis_size("scen")
    n_col = lax.axis_size("col")
    _, depth, block = coupling.shape
    width = hess_diag.shape[0]
    rows = block // n_scen
    piece = width // n_scen
    n_chunk = width // chunk
    n_sub = depth // 2 // sub
    vmem = pltpu.VMEM
    dma = pltpu.SemaphoreType.DMA
    scratch = [
        vmem((depth, depth), F32),
        vmem((depth, block), F32),
        vmem((block, depth), BF16),
        vmem((block, depth), BF16),
        vmem((n_chunk, depth, chunk), F32),
        vmem((depth, chunk), BF16),
        vmem((depth, chunk), BF16),
        vmem((n_chunk, n_scen // 2, 2, rows, chunk), F32),
        vmem((n_chunk, n_scen // 2, rows, chunk), F32),
        vmem((n_chunk, n_scen // 2 - 1, rows, chunk), F32),
        vmem((2, n_scen // 2, 2, piece, width), F32),
        vmem((2, n_scen // 2, piece, width), F32),
        vmem((2, n_scen // 2 - 1, piece, width), F32),
        vmem((n_scen // 2, 2, piece, width), F32),
        vmem((width, width), BF16),
        vmem((width, width), BF16),
        vmem((width, width), F32),
        vmem((width, width), F32),
        vmem((width, width), BF16),
        vmem((width, width), BF16),
        vmem((piece, width), F32),
        vmem((2, rows // piece, piece, width), F32),
        dma((3,)),
        dma((2, (n_chunk + 1) * n_sub)),
        dma((2, (n_chunk + 1) * n_sub)),
        dma((n_chunk,)),
        dma((n_chunk, block // quarter)),
        dma((n_chunk,)),
        dma((n_chunk,)),
        dma((2,)),
        dma((2,)),
        dma((2,)),
        dma((2,)),
        dma(()),
        dma((n_scen // 2 - 1,)),
        dma(()),
        dma((n_scen // 2,)),
        dma(()),
        dma(()),
        dma(()),
        dma((rows // piece,)),
    ]
    return pl.pallas_call(
        functools.partial(kernel, n_scen, n_col, quarter, sub, lag),
        out_shape=(
            jax.ShapeDtypeStruct((rows, width), F32),
            jax.ShapeDtypeStruct((8, 128), F32),
        ),
        in_specs=[
            pl.BlockSpec(memory_space=pl.ANY),
            pl.BlockSpec(memory_space=pl.ANY),
            pl.BlockSpec(memory_space=pltpu.SMEM),
            pl.BlockSpec(memory_space=pltpu.VMEM),
        ],
        out_specs=[pl.BlockSpec(memory_space=pltpu.VMEM)] * 2,
        scratch_shapes=scratch,
        compiler_params=pltpu.CompilerParams(
            collective_id=0, has_side_effects=True, vmem_limit_bytes=50 * 2**20
        ),
    )(inverses, coupling, tile_mask, hess_diag[None, :])


def body(inverses, coupling, tile_mask, hess_diag):
    factor, flag = fused(inverses, coupling, tile_mask, hess_diag)
    return lax.cond(
        flag[0, 0] > 0.5,
        direct_body,
        lambda *_: factor,
        inverses,
        coupling,
        tile_mask,
        hess_diag,
    )


def solution(mesh):
    in_specs = (P("scen", None, None), P("scen", None, "col"), P("scen", None), P())
    out_specs = P(("col", "scen"), None)
    return jax.shard_map(body, mesh=mesh, in_specs=in_specs, out_specs=out_specs, check_vma=False)
```

```python
import functools

import jax
import jax.numpy as jnp
from jax import lax
from jax.experimental import pallas as pl
from jax.experimental.pallas import tpu as pltpu
from jax.sharding import PartitionSpec as P


def from_first(x, axis):
    at = lax.axis_index(axis)
    have = 1
    while have < lax.axis_size(axis):
        pairs = [(i, i + have) for i in range(min(have, lax.axis_size(axis) - have))]
        got = lax.ppermute(x, axis, pairs)
        x = jnp.where(jnp.logical_and(at >= have, at < 2 * have), got, x)
        have *= 2
    return x


def in_blocks(x, dim, size):
    lengths = x.shape
    blocks = x.reshape(*lengths[:dim], size, lengths[dim] // size, *lengths[dim + 1 :])
    return jnp.moveaxis(blocks, dim, 0)


def sum_at_owner(x, axis, dim):
    size = lax.axis_size(axis)
    blocks = lax.all_to_all(in_blocks(x, dim, size), axis, 0, 0, tiled=True)
    return jnp.sum(blocks, axis=0)


def sent_to_all(x, axis):
    size = lax.axis_size(axis)
    return lax.all_to_all(jnp.broadcast_to(x[None], (size, *x.shape)), axis, 0, 0, tiled=True)


def in_order(blocks, dim):
    lengths = list(blocks.shape[1:])
    lengths[dim] *= blocks.shape[0]
    return jnp.moveaxis(blocks, 0, dim).reshape(lengths)


def collect(x, axis, dim):
    blocks = sent_to_all(x, axis)
    return in_order(blocks, dim)


def outer_rows(left, piece):
    return lax.dot_general(
        left,
        piece,
        (((0,), (0,)), ((), ())),
        precision=lax.Precision.HIGHEST,
        preferred_element_type=jnp.float32,
    )


def matmul(left, right):
    return jnp.dot(left, right, precision=lax.Precision.HIGHEST, preferred_element_type=jnp.float32)


def direct_body(inverses, coupling, tile_mask, hess_diag):
    inverse = inverses[0]
    local = coupling[0]
    width = hess_diag.shape[0]
    half = width // 2
    scen_size = lax.axis_size("scen")
    rows = local.shape[1] // scen_size
    row_keep = jnp.repeat(tile_mask[0].astype(jnp.float32), local.shape[0] // tile_mask.shape[1])
    panel = from_first(local[:, :width], "col")
    panel = panel * row_keep[:, None]
    product = matmul(inverse, panel) * row_keep[:, None]
    block = local
    summed = sum_at_owner(outer_rows(block, product), "scen", 0)
    first = lax.axis_index("col") * local.shape[1] + lax.axis_index("scen") * rows
    global_rows = first + jnp.arange(rows, dtype=jnp.int32)
    columns = jnp.arange(width, dtype=jnp.int32)
    schur = summed + jnp.where(columns[None, :] == global_rows[:, None], hess_diag[None, :], 0.0)

    def fetch(stacked, low):
        whole = collect(stacked, "scen", 1)
        block = whole[:, low : low + half]
        return from_first(block, "col")

    identity = jnp.eye(half, dtype=jnp.float32)
    block_one = fetch(schur[None, :, :half], 0)[0]
    chol1 = jnp.linalg.cholesky(block_one)
    inv1 = jax.scipy.linalg.solve_triangular(chol1, identity, lower=True)
    lcol1 = matmul(schur[:, :half], inv1.T)
    own_one = lax.dynamic_slice_in_dim(chol1, jnp.clip(first, 0, half - rows), rows, 0)
    lcol1 = jnp.where(first < half, own_one, lcol1)
    paired = fetch(jnp.stack([schur[:, half:], lcol1]), half)
    lower_b = paired[1]
    update = paired[0] - matmul(lower_b, lower_b.T)
    chol2 = jnp.linalg.cholesky(update)
    inv2 = jax.scipy.linalg.solve_triangular(chol2, identity, lower=True)
    remain = schur[:, half:] - matmul(lcol1, lower_b.T)
    lcol2 = matmul(remain, inv2.T)
    own_two = lax.dynamic_slice_in_dim(chol2, jnp.clip(first - half, 0, half - rows), rows, 0)
    lcol2 = jnp.where(first < width, own_two, lcol2)
    lcol2 = jnp.where(first < half, jnp.zeros_like(lcol2), lcol2)
    return jnp.concatenate([lcol1, lcol2], axis=1)


F32 = jnp.float32
BF16 = jnp.bfloat16
STEPS = 3
SETTLED = 1.6e-5


def split(x):
    high = x.astype(BF16)
    return high, (x - high.astype(F32)).astype(BF16)


def dot(a, b, contract=((1,), (0,))):
    return lax.dot_general(a, b, (contract, ((), ())), preferred_element_type=F32)


def dot3(a, b, contract=((1,), (0,))):
    (a_high, a_low), (b_high, b_low) = a, b
    return (
        dot(a_high, b_high, contract) + dot(a_high, b_low, contract) + dot(a_low, b_high, contract)
    )


NT = ((1,), (1,))


def kernel(
    n_scen,
    n_col,
    quarter,
    sub,
    lag,
    inv_hbm,
    coup_hbm,
    mask_ref,
    hess_ref,
    out_ref,
    flag_ref,
    inv,
    coup,
    high_t,
    low_t,
    prod,
    prod_high,
    prod_low,
    contrib,
    pair_slots,
    slots,
    plane_own,
    plane_pair,
    plane_slots,
    corner,
    scaled_high,
    scaled_low,
    y,
    y_next,
    y_high,
    y_low,
    solve_in,
    solve_out,
    back,
    late_out,
    load_sem,
    ring_send,
    ring_recv,
    pair_send,
    pair_recv,
    sum_send,
    sum_recv,
    plane_pair_send,
    plane_pair_recv,
    plane_send,
    plane_recv,
    fill_send,
    fill_recv,
    fill_pair_send,
    fill_pair_recv,
    in_send,
    in_recv,
    back_send,
    back_recv,
    late_send,
    late_recv,
):
    me = lax.axis_index("scen")
    z = lax.axis_index("col")
    depth = coup.shape[0]
    block = coup.shape[1]
    width = corner.shape[3]
    chunk = prod.shape[2]
    n_chunk = prod.shape[0]
    rows = block // n_scen
    piece = width // n_scen
    owners = width // rows
    tile = depth // mask_ref.shape[1]
    half = depth // 2
    n_sub = half // sub
    nb = width // 2
    n_chip = n_scen // 2
    chip = me // 2
    core = lax.rem(me, 2)
    other = 1 - core
    partner = chip * 2 + other

    barrier = pltpu.get_barrier_semaphore()

    coup_panel = pltpu.make_async_copy(
        coup_hbm.at[0, :, pl.ds(0, width)], coup.at[:, pl.ds(0, width)], load_sem.at[0]
    )
    coup_rest = pltpu.make_async_copy(
        coup_hbm.at[0, :, pl.ds(width, block - width)],
        coup.at[:, pl.ds(width, block - width)],
        load_sem.at[1],
    )
    inv_load = pltpu.make_async_copy(inv_hbm.at[0], inv, load_sem.at[2])
    coup_panel.start()

    @pl.when(z == 0)
    def _():
        inv_load.start()

    coup_rest.start()

    def greet_scen(k, _):
        pl.semaphore_signal(
            barrier,
            inc=1,
            device_id={"scen": lax.rem(me + k, n_scen)},
            device_id_type=pl.DeviceIdType.MESH,
        )
        return 0

    def greet_col(k, _):
        pl.semaphore_signal(
            barrier,
            inc=1,
            device_id={"col": lax.rem(z + k, n_col)},
            device_id_type=pl.DeviceIdType.MESH,
        )
        return 0

    lax.fori_loop(1, n_scen, greet_scen, 0)
    lax.fori_loop(1, n_col, greet_col, 0)
    pl.semaphore_wait(barrier, n_scen + n_col - 2)

    def ring_copy(way, g):
        s = lax.rem(g, n_sub)
        at = prod.at[g // n_sub, pl.ds(pl.multiple_of(way * half + s * sub, sub), sub), :]
        to = lax.rem(z + 1, n_col) if way == 0 else lax.rem(z + n_col - 1, n_col)
        return pltpu.make_async_remote_copy(
            src_ref=at,
            dst_ref=at,
            send_sem=ring_send.at[way, g],
            recv_sem=ring_recv.at[way, g],
            device_id={"col": to},
            device_id_type=pl.DeviceIdType.MESH,
        )

    def transpose_coupling(first, count):
        @pl.loop(0, depth // 128)
        def _(t):
            at = pl.ds(pl.multiple_of(t * 128, 128), 128)
            high, low = split(coup[at, pl.ds(first, count)].T)
            high_t[pl.ds(first, count), at] = high
            low_t[pl.ds(first, count), at] = low

    def split_prod(q):
        high, low = split(prod[q])
        prod_high[...] = high
        prod_low[...] = low

    per = quarter // rows // 2

    def pair_copy(q, r):
        at = pl.ds(pl.multiple_of(r * per, per), per)
        return pltpu.make_async_remote_copy(
            src_ref=contrib.at[q, at, other],
            dst_ref=pair_slots.at[q, at],
            send_sem=pair_send.at[q],
            recv_sem=pair_recv.at[q, r],
            device_id={"scen": partner},
            device_id_type=pl.DeviceIdType.MESH,
        )

    def form(q, r):
        at = pl.ds(pl.multiple_of(r * quarter, quarter), quarter)
        term = dot3((high_t[at, :], low_t[at, :]), (prod_high[...], prod_low[...]))
        contrib[q, pl.ds(pl.multiple_of(r * per, per), per)] = term.reshape(per, 2, rows, chunk)
        pair_copy(q, r).start()

    def pass_on(q, r):
        pair_copy(q, r).wait_recv()
        at = pl.ds(pl.multiple_of(r * per, per), per)
        contrib[q, at, core] = contrib[q, at, core] + pair_slots[q, at]

        def start(k, _):
            to = lax.rem(chip + k, per) + r * per

            @pl.when(to != chip)
            def _():
                pltpu.make_async_remote_copy(
                    src_ref=contrib.at[q, to, core],
                    dst_ref=slots.at[q, lax.rem(chip - to + n_chip, n_chip) - 1],
                    send_sem=sum_send.at[q],
                    recv_sem=sum_recv.at[q],
                    device_id={"scen": to * 2 + core},
                    device_id_type=pl.DeviceIdType.MESH,
                ).start()

            return 0

        lax.fori_loop(0, per, start, 0)

    def own_rows(q):
        own = contrib[q, chip, core]
        return lax.fori_loop(0, n_chip - 1, lambda k, total: total + slots[q, k], own)

    def in_copy(q):
        return pltpu.make_async_remote_copy(
            src_ref=solve_in.at[q, z],
            dst_ref=solve_in.at[q, z],
            send_sem=in_send.at[q],
            recv_sem=in_recv.at[q],
            device_id={"col": 0},
            device_id_type=pl.DeviceIdType.MESH,
        )

    def back_copy(to):
        return pltpu.make_async_remote_copy(
            src_ref=solve_out.at[to],
            dst_ref=back,
            send_sem=back_send,
            recv_sem=back_recv,
            device_id={"col": to},
            device_id_type=pl.DeviceIdType.MESH,
        )

    @pl.when(z == 0)
    def _():
        coup_panel.wait()
        inv_load.wait()
        keep = jnp.concatenate(
            [
                jnp.full((tile, 1), mask_ref[0, t], jnp.int32).astype(F32)
                for t in range(mask_ref.shape[1])
            ],
            axis=0,
        )

        for q in range(n_chunk):
            panel = split(coup[:, pl.ds(q * chunk, chunk)] * keep)
            for r in range(depth // quarter):
                n_half = half // quarter
                r = (r % 2) * n_half + r // 2
                kept = inv[pl.ds(r * quarter, quarter), :]
                scale = keep[r * quarter : (r + 1) * quarter]
                prod[q, pl.ds(r * quarter, quarter), :] = dot3(split(kept), panel) * scale
                way = r // n_half
                for s in range(quarter // sub):
                    ring_copy(way, q * n_sub + (r % n_half) * (quarter // sub) + s).start()

        def plane_pair_copy(part):
            return pltpu.make_async_remote_copy(
                src_ref=plane_own.at[part, :, other],
                dst_ref=plane_pair.at[part],
                send_sem=plane_pair_send.at[part],
                recv_sem=plane_pair_recv.at[part],
                device_id={"scen": partner},
                device_id_type=pl.DeviceIdType.MESH,
            )

        def plane_form(part):
            group = quarter // piece // 2
            for q in range(n_chunk):
                split_prod(q)
                for r in range(width // quarter):
                    at = pl.ds(part * width + r * quarter, quarter)
                    term = dot3((high_t[at, :], low_t[at, :]), (prod_high[...], prod_low[...]))
                    plane_own[part, pl.ds(r * group, group), :, :, pl.ds(q * chunk, chunk)] = (
                        term.reshape(group, 2, piece, chunk)
                    )
            plane_pair_copy(part).start()

        def plane_pass_on(part):
            plane_pair_copy(part).wait_recv()
            step = max(1, n_chip // 4)
            for r in range(0, n_chip, step):
                at = pl.ds(r, step)
                plane_own[part, at, core] = plane_own[part, at, core] + plane_pair[part, at]

            def start(k, _):
                to = lax.rem(chip + k, n_chip)
                pltpu.make_async_remote_copy(
                    src_ref=plane_own.at[part, to, core],
                    dst_ref=plane_slots.at[part, n_chip - 1 - k],
                    send_sem=plane_send.at[part],
                    recv_sem=plane_recv.at[part],
                    device_id={"scen": to * 2 + core},
                    device_id_type=pl.DeviceIdType.MESH,
                ).start()
                return 0

            lax.fori_loop(1, n_chip, start, 0)

        def plane_total(part):
            some = plane_slots.at[part]
            pltpu.make_async_copy(some, some, plane_recv.at[part]).wait()
            return lax.fori_loop(
                0,
                n_chip - 1,
                lambda k, total: total + plane_slots[part, k],
                plane_own[part, chip, core],
            )

        transpose_coupling(0, width)
        plane_form(0)
        coup_rest.wait()
        transpose_coupling(width, block - width)
        plane_pass_on(0)
        plane_form(1)
        total = plane_total(0)
        row = me * piece + lax.broadcasted_iota(jnp.int32, (piece, width), 0)
        column = lax.broadcasted_iota(jnp.int32, (piece, width), 1)
        corner[chip, core] = total + jnp.where(row == column, hess_ref[...], 0.0)

        def fill_copy(k):
            return pltpu.make_async_remote_copy(
                src_ref=corner.at[chip, core],
                dst_ref=corner.at[chip, core],
                send_sem=fill_send,
                recv_sem=fill_recv.at[n_chip - 1 - k],
                device_id={"scen": lax.rem(chip + k, n_chip) * 2 + core},
                device_id_type=pl.DeviceIdType.MESH,
            )

        def hand_copy(k, which):
            at = corner.at[lax.rem(chip + k, n_chip), which]
            return pltpu.make_async_remote_copy(
                src_ref=at,
                dst_ref=at,
                send_sem=fill_pair_send,
                recv_sem=fill_pair_recv.at[k],
                device_id={"scen": partner},
                device_id_type=pl.DeviceIdType.MESH,
            )

        def fill_start(k, _):
            fill_copy(k).start()
            return 0

        hand_copy(0, core).start()
        lax.fori_loop(1, n_chip, fill_start, 0)

        def fill_hand(k, _):
            theirs = corner.at[lax.rem(chip + k, n_chip), core]
            pltpu.make_async_copy(theirs, theirs, fill_recv.at[k - 1]).wait()
            hand_copy(k, core).start()
            return 0

        lax.fori_loop(1, n_chip, fill_hand, 0)

        def hand_wait(k, _):
            hand_copy(k, other).wait_recv()
            return 0

        lax.fori_loop(0, n_chip, hand_wait, 0)
        plane_pass_on(1)

        row = lax.broadcasted_iota(jnp.int32, (width, width), 0)
        column = lax.broadcasted_iota(jnp.int32, (width, width), 1)
        whole = corner[...].reshape(width, width)
        on_diagonal = jnp.where(row == column, whole, 0.0)
        root_row = lax.rsqrt(jnp.sum(on_diagonal, axis=0, keepdims=True))
        root_column = lax.rsqrt(jnp.sum(on_diagonal, axis=1, keepdims=True))
        scaled = whole * root_column * root_row
        high, low = split(scaled)
        scaled_high[...] = high
        scaled_low[...] = low
        y[...] = jnp.where(row == column, 1.0, jnp.where(row > column, -scaled, 0.0))

        for step in range(STEPS):
            high, low = split(y[...])
            y_high[...] = high
            y_low[...] = low
            size = jnp.zeros((1, 1), F32)
            for r in range(2):
                at = pl.ds(r * nb, nb)
                to = pl.ds(0, (r + 1) * nb)
                t = dot3((y_high[at, to], y_low[at, to]), (scaled_high[to, to], scaled_low[to, to]))
                e = dot3(split(t), (y_high[to, to], y_low[to, to]), NT)
                e_row = r * nb + lax.broadcasted_iota(jnp.int32, e.shape, 0)
                e_column = lax.broadcasted_iota(jnp.int32, e.shape, 1)
                e = jnp.where(e_row == e_column, e - 1.0, jnp.where(e_row > e_column, e, 0.0))
                if step == STEPS - 1:
                    size = size + jnp.sum(e * e, keepdims=True)
                e = jnp.where(e_row == e_column, 0.5 * e, e)
                y_next[at, to] = y[at, to] - dot3(split(e), (y_high[to, to], y_low[to, to]))
            for r in range(2):
                at = pl.ds(r * nb, nb)
                to = pl.ds(0, (r + 1) * nb)
                y[at, to] = y_next[at, to]

        bad = jnp.where(size < SETTLED, 0.0, 1.0)
        y_final = split(y[...])

        later = plane_total(1) * root_row
        late_out[1, 0] = dot3(split(later), y_final, NT)
        late_to = owners + me * piece // rows
        late_part = lax.rem(me, rows // piece)

        def late_copy():
            return pltpu.make_async_remote_copy(
                src_ref=late_out.at[1, 0],
                dst_ref=late_out.at[0, late_part],
                send_sem=late_send,
                recv_sem=late_recv.at[late_part],
                device_id={"scen": late_to},
                device_id_type=pl.DeviceIdType.MESH,
            )

        @pl.when(late_to != me)
        def _():
            late_copy().start()

        for q in range(n_chunk):
            rest = solve_in.at[q, pl.ds(1, n_col - 1)]
            pltpu.make_async_copy(rest, rest, in_recv.at[q]).wait()
        given = jnp.concatenate(
            [
                solve_in[q, pl.ds(1, n_col - 1)].reshape((n_col - 1) * rows, chunk)
                for q in range(n_chunk)
            ],
            axis=1,
        )
        given = given * root_row
        solved = dot3(split(given), y_final, NT).reshape(n_col - 1, rows, width)
        solve_out[pl.ds(1, n_col - 1), pl.ds(0, rows), :] = solved
        solve_out[pl.ds(1, n_col - 1), pl.ds(rows, 8), :] = jnp.broadcast_to(
            bad, (n_col - 1, 8, width)
        )

        def back_start(k, _):
            back_copy(n_col // 2 + (k // 2) * (1 - 2 * lax.rem(k, 2))).start()
            return 0

        lax.fori_loop(1, n_col, back_start, 0)

        @pl.when(me < owners)
        def _():
            chips = rows // piece // 2
            given = corner[pl.ds(lax.rem(me, owners) * chips, chips)].reshape(rows, width)
            row = me * rows + lax.broadcasted_iota(jnp.int32, (rows, width), 0)
            column = lax.broadcasted_iota(jnp.int32, (rows, width), 1)
            solved = dot3(split(given * root_row), y_final, NT)
            out_ref[...] = jnp.where(column <= row, solved, 0.0)

        @pl.when(me >= owners)
        def _():
            for part in range(rows // piece):

                @pl.when(jnp.logical_and(late_to == me, late_part == part))
                def _():
                    out_ref[pl.ds(part * piece, piece), :] = late_out[1, 0]

                @pl.when(jnp.logical_not(jnp.logical_and(late_to == me, late_part == part)))
                def _():
                    some = late_out.at[0, part]
                    pltpu.make_async_copy(some, some, late_recv.at[part]).wait()
                    out_ref[pl.ds(part * piece, piece), :] = late_out[0, part]

        flag_ref[...] = jnp.broadcast_to(bad, flag_ref.shape)

        @pl.loop(0, n_chunk * n_sub)
        def _(g):
            ring_copy(0, g).wait_send()
            ring_copy(1, g).wait_send()

        for part in range(2):
            plane_pair_copy(part).wait_send()
            some = plane_slots.at[part]
            pltpu.make_async_copy(some, some, plane_send.at[part]).wait()
        some = corner.at[pl.ds(1, n_chip - 1), 0]
        pltpu.make_async_copy(some, some, fill_send).wait()
        some = corner.at[:, 0]
        pltpu.make_async_copy(some, some, fill_pair_send).wait()

        @pl.when(late_to != me)
        def _():
            late_copy().wait_send()

        some = solve_out.at[pl.ds(1, n_col - 1)]
        pltpu.make_async_copy(some, some, back_send).wait()

    @pl.when(z != 0)
    def _():
        coup_panel.wait()
        coup_rest.wait()
        transpose_coupling(0, block)

        late = lag * jnp.maximum(z - 1, n_col - 1 - z)
        n_piece = n_chunk * n_sub
        n_row = block // quarter

        @pl.loop(0, n_piece + late)
        def _(t):
            g = t - lag * (z - 1)

            @pl.when(jnp.logical_and(g >= 0, g < n_piece))
            def _():
                up = ring_copy(0, g)
                up.wait_recv()

                @pl.when(z < n_col - 1)
                def _():
                    up.start()

            h = t - lag * (n_col - 1 - z)

            @pl.when(jnp.logical_and(h >= 0, h < n_piece))
            def _():
                down = ring_copy(1, h)
                down.wait_recv()

                @pl.when(z > 1)
                def _():
                    down.start()

            done = t - late + 1
            q = done // n_sub - 1
            r = lax.rem(done, n_sub)
            whole = done >= n_sub

            @pl.when(jnp.logical_and(whole, r == 0))
            def _():
                split_prod(q)

            inside = jnp.logical_and(whole, done < n_piece)

            @pl.when(jnp.logical_and(inside, r < n_row))
            def _():
                form(q, r)

            @pl.when(jnp.logical_and(inside, jnp.logical_and(r >= 1, r <= n_row)))
            def _():
                pass_on(q, r - 1)

        form(n_chunk - 1, 0)

        @pl.loop(1, n_row)
        def _(r):
            form(n_chunk - 1, r)
            pass_on(n_chunk - 1, r - 1)

        pass_on(n_chunk - 1, n_row - 1)

        for q in range(n_chunk):
            pltpu.make_async_copy(slots.at[q], slots.at[q], sum_recv.at[q]).wait()
            solve_in[q, z] = own_rows(q)
            in_copy(q).start()

        for q in range(n_chunk):

            pltpu.make_async_copy(slots.at[q], slots.at[q], sum_send.at[q]).wait()
            pltpu.make_async_copy(pair_slots.at[q], pair_slots.at[q], pair_send.at[q]).wait()
        for q in range(n_chunk):
            in_copy(q).wait_send()

        @pl.loop(0, n_piece)
        def _(g):
            @pl.when(z < n_col - 1)
            def _():
                ring_copy(0, g).wait_send()

            @pl.when(z > 1)
            def _():
                ring_copy(1, g).wait_send()

        pltpu.make_async_copy(back, back, back_recv).wait()
        out_ref[...] = back[pl.ds(0, rows), :]
        flag_ref[...] = back[pl.ds(rows, 8), pl.ds(0, 128)]


def fused(inverses, coupling, tile_mask, hess_diag, quarter=256, chunk=128, sub=64, lag=5):
    n_scen = lax.axis_size("scen")
    n_col = lax.axis_size("col")
    _, depth, block = coupling.shape
    width = hess_diag.shape[0]
    rows = block // n_scen
    piece = width // n_scen
    n_chunk = width // chunk
    n_sub = depth // 2 // sub
    vmem = pltpu.VMEM
    dma = pltpu.SemaphoreType.DMA
    scratch = [
        vmem((depth, depth), F32),
        vmem((depth, block), F32),
        vmem((block, depth), BF16),
        vmem((block, depth), BF16),
        vmem((n_chunk, depth, chunk), F32),
        vmem((depth, chunk), BF16),
        vmem((depth, chunk), BF16),
        vmem((n_chunk, n_scen // 2, 2, rows, chunk), F32),
        vmem((n_chunk, n_scen // 2, rows, chunk), F32),
        vmem((n_chunk, n_scen // 2 - 1, rows, chunk), F32),
        vmem((2, n_scen // 2, 2, piece, width), F32),
        vmem((2, n_scen // 2, piece, width), F32),
        vmem((2, n_scen // 2 - 1, piece, width), F32),
        vmem((n_scen // 2, 2, piece, width), F32),
        vmem((width, width), BF16),
        vmem((width, width), BF16),
        vmem((width, width), F32),
        vmem((width, width), F32),
        vmem((width, width), BF16),
        vmem((width, width), BF16),
        vmem((n_chunk, n_col, rows, chunk), F32),
        vmem((n_col, rows + 8, width), F32),
        vmem((rows + 8, width), F32),
        vmem((2, rows // piece, piece, width), F32),
        dma((3,)),
        dma((2, n_chunk * n_sub)),
        dma((2, n_chunk * n_sub)),
        dma((n_chunk,)),
        dma((n_chunk, block // quarter)),
        dma((n_chunk,)),
        dma((n_chunk,)),
        dma((2,)),
        dma((2,)),
        dma((2,)),
        dma((2,)),
        dma(()),
        dma((n_scen // 2 - 1,)),
        dma(()),
        dma((n_scen // 2,)),
        dma((n_chunk,)),
        dma((n_chunk,)),
        dma(()),
        dma(()),
        dma(()),
        dma((rows // piece,)),
    ]
    return pl.pallas_call(
        functools.partial(kernel, n_scen, n_col, quarter, sub, lag),
        out_shape=(
            jax.ShapeDtypeStruct((rows, width), F32),
            jax.ShapeDtypeStruct((8, 128), F32),
        ),
        in_specs=[
            pl.BlockSpec(memory_space=pl.ANY),
            pl.BlockSpec(memory_space=pl.ANY),
            pl.BlockSpec(memory_space=pltpu.SMEM),
            pl.BlockSpec(memory_space=pltpu.VMEM),
        ],
        out_specs=[pl.BlockSpec(memory_space=pltpu.VMEM)] * 2,
        scratch_shapes=scratch,
        compiler_params=pltpu.CompilerParams(
            collective_id=0, has_side_effects=True, vmem_limit_bytes=50 * 2**20
        ),
    )(inverses, coupling, tile_mask, hess_diag[None, :])


def body(inverses, coupling, tile_mask, hess_diag):
    factor, flag = fused(inverses, coupling, tile_mask, hess_diag)
    return lax.cond(
        flag[0, 0] > 0.5,
        direct_body,
        lambda *_: factor,
        inverses,
        coupling,
        tile_mask,
        hess_diag,
    )


def solution(mesh):
    in_specs = (P("scen", None, None), P("scen", None, "col"), P("scen", None), P())
    out_specs = P(("col", "scen"), None)
    return jax.shard_map(body, mesh=mesh, in_specs=in_specs, out_specs=out_specs, check_vma=False)
```
